256 devices in a mesh: tensor: 8 (over x, z_lo), member: 4 (over z_hi), image: 8 (over y, core).
Axes of the slice: x: 4, y: 4, z: 8 (z_hi: 4, z_lo: 2; z = z_hi * 2 + z_lo), core: 2. Of those that a mesh axis runs over, the one named last changes fastest.
Arguments:
- acts: bfloat16 [4, 8, 1024, 3200], P('member', 'image', 'tensor'), may hold values from -12 to 12
- perturb: bfloat16 [1024, 3200], P(('tensor', 'member', 'image')), may hold values from -1.796875 to 1.796875
- dy: bfloat16 [4, 8, 1024, 3200], P('member', 'image', 'tensor'), may hold values from -1.5 to 1.5
- norm_gain: float32 [4, 3200], P('member'), may hold values from 0.5 to 1.5
- w_qkv: bfloat16 [4, 3200, 16, 3, 128], P('member', None, 'tensor'), may hold values from -4 to 4
- w_out: bfloat16 [4, 16, 128, 3200], P('member', 'tensor'), may hold values from -0.375 to 0.375
Outputs:
- grad_perturb: float32 [1024, 3200], P(('tensor', 'member', 'image'))
The draws below stay inside these ranges and needn't reach their ends.
All inputs are finite; a program needn't handle non-finite values.
Results may differ from the reference program's by a relative error of at most 0.013.
The reference program's roundings to bfloat16 on the way count: a program that leaves them out, or rounds other values in their place, can miss the bound.
Values may be sent and summed in bfloat16 or wider, within the bound.
No kernel may reach another device: no remote copies, remote signals or barrier semaphores. Data moves between devices by JAX's collectives and lax.ppermute only.
A program may use at most 128 MiB of HBM per device.

```python
import math
import jax
import jax.numpy as jnp
from jax import lax

D = 3200
E = 128
H = 16
SEQ = 1024
HEADS_DEV = 2
MEMBERS = 4
IMAGES = 8
N_TENSOR = 8


def draw_acts(key, part):
    keys = jax.random.split(key, 3)
    shape = (MEMBERS, IMAGES, SEQ, D)
    feature_scale = jnp.exp(jax.random.uniform(keys[0], (MEMBERS, 1, 1, D), minval=0.0, maxval=math.log(10.0)))
    row_scale = jnp.exp(jax.random.uniform(keys[1], (MEMBERS, IMAGES, SEQ, 1), minval=0.0, maxval=math.log(10.0)))
    base = jnp.clip(jax.random.normal(keys[2], shape), -4.0, 4.0)
    return (0.03 * base * feature_scale * row_scale).astype(jnp.bfloat16)


def draw_w_qkv(key, part):
    keys = jax.random.split(key, 1)
    shape = (MEMBERS, D, H, 3, E)
    weights = jnp.clip(jax.random.normal(keys[0], shape), -5.0, 5.0) * (1.4 * D ** (-0.5))
    return weights.astype(jnp.bfloat16)


def levels(own_key, extent, shards, smallest, high):
    gain, own = 1.0, jax.random.fold_in(own_key, 6)
    for dim, parts in shards:
        heights = jnp.exp(jax.random.uniform(jax.random.fold_in(own, dim), (parts,), jnp.float32, smallest / len(shards), high / len(shards)))
        gain = gain * jnp.repeat(heights, extent[dim] // parts).reshape([-1 if axis == dim else 1 for axis in range(len(extent))])
    return gain


def centred(rng, shape, deviation, reach, pieces=(), held_as=jnp.bfloat16):
    drawn = deviation * jax.random.normal(rng, shape, jnp.float32)
    if pieces:
        drawn = drawn * levels(rng, shape, pieces, -0.22, 0.18)
    return jnp.clip(drawn, -reach, reach).astype(held_as)


def setup_inputs(seed: int = 0) -> dict:
    streams_of = jax.random.split(jax.random.key(seed), 7)
    acts = draw_acts(jax.random.fold_in(streams_of[6], 71), 0)
    perturb = centred(streams_of[1], (SEQ, D), 0.3, 1.796875, ((0, 256),))
    dy = centred(streams_of[2], (MEMBERS, IMAGES, SEQ, D), 0.25, 1.5, ((0, 4), (1, 8), (2, 8)))
    norm_gain = jnp.clip(1.0 + 0.1 * jax.random.normal(streams_of[3], (MEMBERS, D), jnp.float32), 0.5, 1.5)
    w_qkv = draw_w_qkv(jax.random.fold_in(streams_of[6], 71), 0)
    w_out = centred(streams_of[5], (MEMBERS, H, E, D), (H * E // 8) ** -0.5, 0.375, ((0, 4), (1, 8)))
    return {"acts": acts, "perturb": perturb, "dy": dy, "norm_gain": norm_gain, "w_qkv": w_qkv, "w_out": w_out}


def normalize(row_block):
    floats = row_block.astype(jnp.float32)
    spread = jnp.sqrt(lax.optimization_barrier(jnp.mean(floats * floats, axis=-1, keepdims=True)) + 1e-06)
    return (floats / spread, spread)

def norm_back(normed_grad, row_block, gains, upstream):
    scaled_rows, spread = normalize(row_block)
    weighted = gains * normed_grad
    centre = lax.optimization_barrier(jnp.mean(scaled_rows * weighted, axis=-1, keepdims=True))
    return upstream.astype(jnp.float32) + (weighted - scaled_rows * centre) / spread

def member_image(inputs, upstream, gains, w_qkv, w_out):
    length, features = inputs.shape
    score_scale = E ** (-0.5)
    w_mat = w_qkv.reshape(features, H * 3 * E)
    scaled_rows, spread = normalize(inputs)
    normed = (scaled_rows * gains).astype(jnp.bfloat16)
    packed = jnp.dot(normed, w_mat, preferred_element_type=jnp.float32).astype(jnp.bfloat16)
    packed = packed.reshape(length, H, 3, E)
    query = packed[:, :, 0].astype(jnp.float32)
    keys = packed[:, :, 1].astype(jnp.float32)
    values = packed[:, :, 2].astype(jnp.float32)
    heads_up = jnp.dot(upstream, w_out.reshape(H * E, features).T, preferred_element_type=jnp.float32)
    heads_up = heads_up.astype(jnp.bfloat16).reshape(length, H, E).astype(jnp.float32)
    scores = jnp.einsum('qhe,khe->hqk', query, keys) * score_scale
    peak = lax.optimization_barrier(jnp.max(scores, axis=-1, keepdims=True))
    expo = jnp.exp(scores - peak)
    attention = expo / lax.optimization_barrier(jnp.sum(expo, axis=-1, keepdims=True))
    rounded = attention.astype(jnp.bfloat16).astype(jnp.float32)
    through = jnp.einsum('qhe,khe->hqk', heads_up, values)
    value_grad = jnp.einsum('hqk,qhe->khe', rounded, heads_up).astype(jnp.bfloat16)
    centre = lax.optimization_barrier(jnp.sum(attention * through, axis=-1, keepdims=True))
    score_grad = (attention * (through - centre) * score_scale).astype(jnp.bfloat16).astype(jnp.float32)
    query_grad = jnp.einsum('hqk,khe->qhe', score_grad, keys).astype(jnp.bfloat16)
    key_grad = jnp.einsum('hqk,qhe->khe', score_grad, query).astype(jnp.bfloat16)
    packed_back = jnp.stack([query_grad, key_grad, value_grad], axis=2).reshape(length, H * 3 * E)
    group_cols = HEADS_DEV * 3 * E
    normed_grad = jnp.zeros((length, features), jnp.float32)
    for group in range(N_TENSOR):
        grad_cols = packed_back[:, group * group_cols:(group + 1) * group_cols]
        weight_cols = w_mat[:, group * group_cols:(group + 1) * group_cols]
        partial_value = jnp.dot(grad_cols, weight_cols.T, preferred_element_type=jnp.float32)
        partial_value = lax.optimization_barrier(partial_value.astype(jnp.bfloat16)).astype(jnp.float32)
        normed_grad = normed_grad + partial_value
    return norm_back(normed_grad, inputs, gains, upstream)

def reference(acts, perturb, dy, norm_gain, w_qkv, w_out):
    inputs = (acts.astype(jnp.float32) + perturb.astype(jnp.float32)[None, None]).astype(jnp.bfloat16)

    def over_members(carry, member_data):
        member_inputs, member_dy, gains, member_qkv, member_out = member_data

        def over_images(inner, image_data):
            image_inputs, image_dy = image_data
            return (inner + member_image(image_inputs, image_dy, gains, member_qkv, member_out), None)
        carry, unused = lax.scan(over_images, carry, (member_inputs, member_dy))
        return (carry, None)
    start_sum = jnp.zeros((SEQ, D), jnp.float32)
    result, unused = lax.scan(over_members, start_sum, (inputs, dy, norm_gain, w_qkv, w_out))
    return result
```

```python
import math

import jax
import jax.numpy as jnp
from jax import lax
from jax.sharding import PartitionSpec as P

AXES = ("tensor", "member", "image")
BF = jnp.bfloat16
F32 = jnp.float32


def routes(move):
    pairs = []
    for x in range(4):
        for zl in range(2):
            for zh in range(4):
                for y in range(4):
                    for c in range(2):
                        nx, nzl, nzh, ny, nc = move(x, zl, zh, y, c)
                        pairs.append(
                            (
                                ((x * 2 + zl) * 4 + zh) * 8 + y * 2 + c,
                                (((nx % 4) * 2 + nzl) * 4 + nzh % 4) * 8 + (ny % 4) * 2 + nc,
                            )
                        )
    return pairs


SWAP = routes(lambda x, zl, zh, y, c: (x, c, zh, y, zl))
CORE = routes(lambda x, zl, zh, y, c: (x, zl, zh, y, 1 - c))
ZL = routes(lambda x, zl, zh, y, c: (x, 1 - zl, zh, y, c))
X = {d: routes(lambda x, zl, zh, y, c, d=d: (x + d, zl, zh, y, c)) for d in (-1, 1, 2)}
Y = {d: routes(lambda x, zl, zh, y, c, d=d: (x, zl, zh, y + d, c)) for d in (-1, 1, 2)}
Z = {d: routes(lambda x, zl, zh, y, c, d=d: (x, zl, zh + d, y, c)) for d in (-1, 1, 2)}


def send(value, pairs):
    return lax.ppermute(value, AXES, pairs)


def ring_gather(value, ring, own):
    offsets = {0: value, 3: send(value, ring[1]), 1: send(value, ring[-1]), 2: send(value, ring[2])}
    out = []
    for place in range(4):
        step = (place - own) % 4
        piece = offsets[0]
        for offset in (1, 2, 3):
            piece = jnp.where(step == offset, offsets[offset], piece)
        out.append(piece)
    return jnp.stack(out)


def ring_blocks(block):
    half = block.shape[0] // 2
    left = send(block, X[1])
    right = send(block, X[-1])
    far = jnp.concatenate([send(left[:half], X[1]), send(right[half:], X[-1])], axis=0)
    return left, right, far


def spread_of(rows):
    floats = rows.astype(F32)
    return jnp.sqrt(jnp.mean(floats * floats, axis=-1, keepdims=True) + 1e-06)


def head_grads(query, keys, values, upstream, score_scale):
    scores = jnp.einsum("qe,ke->qk", query, keys, preferred_element_type=F32) * score_scale
    peak = jnp.max(scores, axis=-1, keepdims=True)
    expo = jnp.exp(scores - peak)
    attention = expo / jnp.sum(expo, axis=-1, keepdims=True)
    rounded = attention.astype(BF)
    through = jnp.einsum("qe,ke->qk", upstream, values, preferred_element_type=F32)
    value_grad = jnp.einsum("qk,qe->ke", rounded, upstream, preferred_element_type=F32).astype(BF)
    centre = jnp.sum(attention * through, axis=-1, keepdims=True)
    score_grad = (attention * (through - centre) * score_scale).astype(BF)
    query_grad = jnp.einsum("qk,ke->qe", score_grad, keys, preferred_element_type=F32).astype(BF)
    key_grad = jnp.einsum("qk,qe->ke", score_grad, query, preferred_element_type=F32).astype(BF)
    return (query_grad, key_grad, value_grad)


def matmul_t(left, right):
    return lax.dot_general(left, right, (((1,), (1,)), ((), ())), preferred_element_type=F32)


def on_device(acts, perturb, dy, norm_gain, w_qkv, w_out):
    image = lax.axis_index("image")
    own_y, core = image // 2, image % 2
    member = lax.axis_index("member")
    features = acts.shape[3]
    heads, head_size = w_qkv.shape[2], w_qkv.shape[4]
    gains = norm_gain[0]
    score_scale = 1.0 / math.sqrt(head_size)
    first = core == 0

    dy_own = send(dy[0, 0], SWAP)
    dy_left, dy_right, dy_far = ring_blocks(dy_own)

    rows = ring_gather(perturb, Y, own_y)
    rows = ring_gather(rows, Z, member)
    other = send(rows, CORE)
    shared = jnp.stack(
        [jnp.where(first, rows, other), jnp.where(first, other, rows)], axis=2
    ).reshape(-1, features)
    inputs = (acts[0, 0].astype(F32) + shared.astype(F32)).astype(BF)
    in_own = send(inputs, SWAP)
    in_left, in_right, in_far = ring_blocks(in_own)

    def other_weights(weight):
        piece = weight.shape[0] // 8
        mine = lax.dynamic_slice_in_dim(weight, image * piece, piece, 0)
        gathered = ring_gather(send(mine, ZL), Y, own_y)
        beside = send(gathered, CORE)
        return jnp.stack(
            [jnp.where(first, gathered, beside), jnp.where(first, beside, gathered)], axis=1
        ).reshape(weight.shape)

    w_back = w_out[0].reshape(heads * head_size, features)
    w_mat = w_qkv[0].reshape(features, heads * 3 * head_size).T
    w_back_other = other_weights(w_back)
    w_mat_other = other_weights(w_mat)

    near_dy = jnp.concatenate([dy_own, dy_left, dy_right], axis=0)
    near_in = jnp.concatenate([in_own, in_left, in_right], axis=0)

    def projected(rows_dy, rows_in):
        spread = spread_of(rows_in)
        normed = (rows_in.astype(F32) / spread * gains).astype(BF)
        return [
            matmul_t(normed, w_mat).astype(BF),
            matmul_t(normed, w_mat_other).astype(BF),
            matmul_t(rows_dy, w_back).astype(BF),
            matmul_t(rows_dy, w_back_other).astype(BF),
        ]

    near, far = projected(near_dy, near_in), projected(dy_far, in_far)
    packed, packed_other, up, up_other = [
        jnp.concatenate([a, b], axis=0) for a, b in zip(near, far, strict=True)
    ]
    both = jnp.concatenate([packed, up], axis=1)
    both_other = jnp.concatenate([packed_other, up_other], axis=1)
    keep = jnp.where(first, both, both_other)
    came = send(jnp.where(first, both_other, both), CORE)
    table = jnp.concatenate([keep, came], axis=0)
    pieces = []
    for head in range(heads):
        at = [(head * 3 + slot) * head_size for slot in range(3)] + [
            (heads * 3 + head) * head_size
        ]
        query, keys, values, upstream = [table[:, a : a + head_size] for a in at]
        pieces.extend(head_grads(query, keys, values, upstream, score_scale))
    grads = jnp.concatenate(pieces, axis=1)
    count = grads.shape[0] // 2
    mine, came = grads[:count], send(grads[count:], CORE)
    grads_own = jnp.where(first, mine, came)
    grads_other = jnp.where(first, came, mine)

    def partial(values, weight):
        part = lax.dot_general(
            values, weight, (((1,), (0,)), ((), ())), preferred_element_type=F32
        )
        return lax.optimization_barrier(part.astype(BF)).astype(F32)

    normed_grad = partial(grads_own, w_mat) + partial(grads_other, w_mat_other)
    rows_in = jnp.concatenate([in_own, in_left, in_right, in_far], axis=0)
    spread = spread_of(rows_in)
    unit = rows_in.astype(F32) / spread
    weighted = gains * normed_grad
    centre = jnp.mean(unit * weighted, axis=-1, keepdims=True)
    result = (weighted - unit * centre) / spread
    blocks = dy_own.shape[0]
    result = jnp.concatenate([result[:blocks] + dy_own.astype(F32), result[blocks:]], axis=0)
    result = result.astype(BF).reshape(4, 4, 4, 8, features)

    def over_x(value):
        total = value[0].astype(F32)
        for place, step in ((1, -1), (2, 1), (3, 2)):
            total = total + send(value[place], X[step]).astype(F32)
        return total

    def over(value, ring, own, dim):
        total = lax.dynamic_index_in_dim(value, own, dim, keepdims=False).astype(F32)
        for step in (2, 1, -1):
            piece = lax.dynamic_index_in_dim(value, (own + step) % 4, dim, keepdims=False)
            total = total + send(piece, ring[step]).astype(F32)
        return total

    cut = 1664
    part_a = over_x(result[..., :cut])
    part_b = over(result[..., cut:], Y, own_y, 2)
    part_a = over(part_a.astype(BF), Y, own_y, 1)
    part_b = over_x(part_b.astype(BF))
    total = jnp.concatenate([part_a, part_b], axis=-1)
    total = over(total, Z, member, 0)
    total = send(total, SWAP).reshape(2, 4, features)
    low, high = total[0], total[1]
    return jnp.where(first, low, high) + send(jnp.where(first, high, low), CORE)


def solution(mesh):
    in_specs = (
        P("member", "image", "tensor", None),
        P(("tensor", "member", "image"), None),
        P("member", "image", "tensor", None),
        P("member", None),
        P("member", None, "tensor", None, None),
        P("member", "tensor", None, None),
    )
    out_specs = P(("tensor", "member", "image"), None)
    return jax.shard_map(
        on_device, mesh=mesh, in_specs=in_specs, out_specs=out_specs, check_vma=False
    )
```

```python
import math

import jax
import jax.numpy as jnp
from jax import lax
from jax.sharding import PartitionSpec as P

AXES = ("tensor", "member", "image")
BF = jnp.bfloat16
F32 = jnp.float32


def routes(move):
    pairs = []
    for x in range(4):
        for zl in range(2):
            for zh in range(4):
                for y in range(4):
                    for c in range(2):
                        nx, nzl, nzh, ny, nc = move(x, zl, zh, y, c)
                        pairs.append(
                            (
                                ((x * 2 + zl) * 4 + zh) * 8 + y * 2 + c,
                                (((nx % 4) * 2 + nzl) * 4 + nzh % 4) * 8 + (ny % 4) * 2 + nc,
                            )
                        )
    return pairs


SWAP = routes(lambda x, zl, zh, y, c: (x, c, zh, y, zl))
CORE = routes(lambda x, zl, zh, y, c: (x, zl, zh, y, 1 - c))
ZL = routes(lambda x, zl, zh, y, c: (x, 1 - zl, zh, y, c))
X = {d: routes(lambda x, zl, zh, y, c, d=d: (x + d, zl, zh, y, c)) for d in (-1, 1, 2)}

Y = {d: routes(lambda x, zl, zh, y, c, d=d: (x, zl, zh, y + d, c)) for d in (-1, 1, 2)}


def send(value, pairs):
    return lax.ppermute(value, AXES, pairs)


def exchange(value, axis):
    groups = None if axis == "member" else [[0, 2, 4, 6], [1, 3, 5, 7]]
    return lax.all_to_all(value, axis, 0, 0, axis_index_groups=groups)


def ring_blocks(block):
    half = block.shape[0] // 2
    left = send(block, X[1])
    right = send(block, X[-1])
    far = jnp.concatenate([send(left[:half], X[1]), send(right[half:], X[-1])], axis=0)
    return left, right, far


def placed(pieces, own):
    blank = jnp.zeros((4, *pieces[0].shape), pieces[0].dtype)
    for piece, step in zip(pieces, (0, 3, 1, 2), strict=True):
        blank = lax.dynamic_update_index_in_dim(blank, piece, (own + step) % 4, 0)
    return blank.reshape(-1, *pieces[0].shape[1:])


def spread_of(rows):
    floats = rows.astype(F32)
    return jnp.sqrt(jnp.mean(floats * floats, axis=-1, keepdims=True) + 1e-06)


def head_grads(query, keys, values, upstream, score_scale):
    scores = jnp.einsum("qe,ke->qk", query, keys, preferred_element_type=F32) * score_scale
    peak = jnp.max(scores, axis=-1, keepdims=True)
    expo = jnp.exp(scores - peak)
    attention = expo / jnp.sum(expo, axis=-1, keepdims=True)
    rounded = attention.astype(BF)
    through = jnp.einsum("qe,ke->qk", upstream, values, preferred_element_type=F32)
    value_grad = jnp.einsum("qk,qe->ke", rounded, upstream, preferred_element_type=F32).astype(BF)
    centre = jnp.sum(attention * through, axis=-1, keepdims=True)
    score_grad = (attention * (through - centre) * score_scale).astype(BF)
    query_grad = jnp.einsum("qk,ke->qe", score_grad, keys, preferred_element_type=F32).astype(BF)
    key_grad = jnp.einsum("qk,qe->ke", score_grad, query, preferred_element_type=F32).astype(BF)
    return (query_grad, key_grad, value_grad)


def matmul_t(left, right):
    return lax.dot_general(left, right, (((1,), (1,)), ((), ())), preferred_element_type=F32)


def on_device(acts, perturb, dy, norm_gain, w_qkv, w_out):
    image = lax.axis_index("image")
    own_x, own_y, core = lax.axis_index("tensor") // 2, image // 2, image % 2
    block = dy.shape[2]
    features = acts.shape[3]
    heads, head_size = w_qkv.shape[2], w_qkv.shape[4]
    gains = norm_gain[0]
    score_scale = 1.0 / math.sqrt(head_size)
    first = core == 0

    dy_own = send(dy[0, 0], SWAP)

    shared = lax.all_to_all(
        jnp.broadcast_to(perturb, (32, *perturb.shape)), ("member", "image"), 0, 0
    ).reshape(-1, features)
    inputs = (acts[0, 0].astype(F32) + shared.astype(F32)).astype(BF)
    in_own = send(inputs, SWAP)
    in_left, in_right, in_far = ring_blocks(in_own)

    w_back = w_out[0].reshape(heads * head_size, features)
    w_mat = w_qkv[0].reshape(features, heads * 3 * head_size).T
    split = w_mat.shape[0] // 8
    split_back = w_back.shape[0] // 8
    mine = jnp.concatenate(
        [
            lax.dynamic_slice_in_dim(w_mat, image * split, split, 0),
            lax.dynamic_slice_in_dim(w_back, image * split_back, split_back, 0),
        ],
        axis=0,
    )
    mine, dy_own = lax.optimization_barrier((mine, dy_own))
    mine = send(mine, ZL)
    gathered = exchange(jnp.broadcast_to(mine, (4, *mine.shape)), "image")
    beside = send(gathered, CORE)
    w_mat_other, w_back_other = [
        jnp.stack(
            [
                jnp.where(first, gathered[:, part], beside[:, part]),
                jnp.where(first, beside[:, part], gathered[:, part]),
            ],
            axis=1,
        ).reshape(-1, features)
        for part in (slice(0, split), slice(split, split + split_back))
    ]

    dy_left, dy_right, dy_far = ring_blocks(dy_own)
    near_dy = jnp.concatenate([dy_own, dy_left, dy_right], axis=0)
    near_in = jnp.concatenate([in_own, in_left, in_right], axis=0)

    def projected(rows_dy, rows_in):
        spread = spread_of(rows_in)
        normed = (rows_in.astype(F32) / spread * gains).astype(BF)
        return [
            matmul_t(normed, w_mat).astype(BF),
            matmul_t(normed, w_mat_other).astype(BF),
            matmul_t(rows_dy, w_back).astype(BF),
            matmul_t(rows_dy, w_back_other).astype(BF),
        ]

    near, far = projected(near_dy, near_in), projected(dy_far, in_far)
    packed, packed_other, up, up_other = [
        placed([a[:block], a[block : 2 * block], a[2 * block :], b], own_x)
        for a, b in zip(near, far, strict=True)
    ]
    both = jnp.concatenate([packed, up], axis=1)
    both_other = jnp.concatenate([packed_other, up_other], axis=1)
    keep = jnp.where(first, both, both_other)
    came = send(jnp.where(first, both_other, both), CORE)
    table = jnp.concatenate([keep, came], axis=0)
    pieces = []
    for head in range(heads):
        at = [(head * 3 + slot) * head_size for slot in range(3)] + [
            (heads * 3 + head) * head_size
        ]
        query, keys, values, upstream = [table[:, a : a + head_size] for a in at]
        pieces.extend(head_grads(query, keys, values, upstream, score_scale))
    grads = jnp.concatenate(pieces, axis=1)
    count = grads.shape[0] // 2
    mine, came = grads[:count], send(grads[count:], CORE)
    grads_own = jnp.where(first, mine, came)
    grads_other = jnp.where(first, came, mine)

    def partial(values, weight):
        part = lax.dot_general(
            values, weight, (((1,), (0,)), ((), ())), preferred_element_type=F32
        )
        return lax.optimization_barrier(part.astype(BF)).astype(F32)

    normed_grad = partial(grads_own, w_mat) + partial(grads_other, w_mat_other)
    rows_in = placed([in_own, in_left, in_right, in_far], own_x)
    spread = spread_of(rows_in)
    unit = rows_in.astype(F32) / spread
    weighted = gains * normed_grad
    centre = jnp.mean(unit * weighted, axis=-1, keepdims=True)
    result = (weighted - unit * centre) / spread
    result = result.reshape(4, block, features) + jnp.where(
        lax.iota(jnp.int32, 4)[:, None, None] == own_x, dy_own.astype(F32), 0.0
    )
    result = result.astype(BF).reshape(4, 4, 4, 8, features)
    cut = 1664

    def summed(value, axis):
        return jnp.sum(exchange(value, axis).astype(F32), axis=0)

    def over_y(value, dim):
        total = lax.dynamic_index_in_dim(value, own_y, dim, keepdims=False).astype(F32)
        for step in (2, 1, -1):
            piece = lax.dynamic_index_in_dim(value, (own_y + step) % 4, dim, keepdims=False)
            total = total + send(piece, Y[step]).astype(F32)
        return total

    part_a = summed(result[..., :cut], "tensor")
    part_b = over_y(result[..., cut:], 2)
    part_a = over_y(part_a.astype(BF), 1)
    part_b = summed(part_b.astype(BF), "tensor")
    total = jnp.concatenate([part_a, part_b], axis=-1)
    total = summed(total, "member")
    total = send(total, SWAP).reshape(2, 4, features)
    low, high = total[0], total[1]
    return jnp.where(first, low, high) + send(jnp.where(first, high, low), CORE)


def solution(mesh):
    in_specs = (
        P("member", "image", "tensor", None),
        P(("tensor", "member", "image"), None),
        P("member", "image", "tensor", None),
        P("member", None),
        P("member", None, "tensor", None, None),
        P("member", "tensor", None, None),
    )
    out_specs = P(("tensor", "member", "image"), None)
    return jax.shard_map(
        on_device, mesh=mesh, in_specs=in_specs, out_specs=out_specs, check_vma=False
    )
```

```python
import math

import jax
import jax.numpy as jnp
from jax import lax
from jax.sharding import PartitionSpec as P

AXES = ("tensor", "member", "image")
BF = jnp.bfloat16
F32 = jnp.float32


def routes(move):
    pairs = []
    for x in range(4):
        for zl in range(2):
            for zh in range(4):
                for y in range(4):
                    for c in range(2):
                        nx, nzl, nzh, ny, nc = move(x, zl, zh, y, c)
                        pairs.append(
                            (
                                ((x * 2 + zl) * 4 + zh) * 8 + y * 2 + c,
                                (((nx % 4) * 2 + nzl) * 4 + nzh % 4) * 8 + (ny % 4) * 2 + nc,
                            )
                        )
    return pairs


SWAP = routes(lambda x, zl, zh, y, c: (x, c, zh, y, zl))
CORE = routes(lambda x, zl, zh, y, c: (x, zl, zh, y, 1 - c))
ZL = routes(lambda x, zl, zh, y, c: (x, 1 - zl, zh, y, c))
X = {d: routes(lambda x, zl, zh, y, c, d=d: (x + d, zl, zh, y, c)) for d in (-1, 1, 2)}

Y = {d: routes(lambda x, zl, zh, y, c, d=d: (x, zl, zh, y + d, c)) for d in (-1, 1, 2)}


def send(value, pairs):
    return lax.ppermute(value, AXES, pairs)


def after(value, *seen):
    return lax.optimization_barrier((value, *seen))[0]


def exchange(value, axis):
    groups = None if axis == "member" else [[0, 2, 4, 6], [1, 3, 5, 7]]
    return lax.all_to_all(value, axis, 0, 0, axis_index_groups=groups)


def ring_blocks(block):
    half = block.shape[0] // 2
    left = send(block, X[1])
    right = send(block, X[-1])
    return left, right, [send(left[:half], X[1]), send(right[half:], X[-1])]


def placed(pieces, own):
    blank = jnp.zeros((4, *pieces[0].shape), pieces[0].dtype)
    for piece, step in zip(pieces, (0, 3, 1, 2), strict=True):
        blank = lax.dynamic_update_index_in_dim(blank, piece, (own + step) % 4, 0)
    return blank.reshape(-1, *pieces[0].shape[1:])


def spread_of(rows):
    floats = rows.astype(F32)
    return jnp.sqrt(jnp.mean(floats * floats, axis=-1, keepdims=True) + 1e-06)


def head_grads(query, keys, values, upstream, score_scale):
    scores = jnp.einsum("qe,ke->qk", query, keys, preferred_element_type=F32) * score_scale
    peak = jnp.max(scores, axis=-1, keepdims=True)
    expo = jnp.exp(scores - peak)
    attention = expo / jnp.sum(expo, axis=-1, keepdims=True)
    rounded = attention.astype(BF)
    through = jnp.einsum("qe,ke->qk", upstream, values, preferred_element_type=F32)
    value_grad = jnp.einsum("qk,qe->ke", rounded, upstream, preferred_element_type=F32).astype(BF)
    centre = jnp.sum(attention * through, axis=-1, keepdims=True)
    score_grad = (attention * (through - centre) * score_scale).astype(BF)
    query_grad = jnp.einsum("qk,ke->qe", score_grad, keys, preferred_element_type=F32).astype(BF)
    key_grad = jnp.einsum("qk,qe->ke", score_grad, query, preferred_element_type=F32).astype(BF)
    return (query_grad, key_grad, value_grad)


def matmul_t(left, right):
    return lax.dot_general(left, right, (((1,), (1,)), ((), ())), preferred_element_type=F32)


def on_device(acts, perturb, dy, norm_gain, w_qkv, w_out):
    image = lax.axis_index("image")
    own_x, own_y, core = lax.axis_index("tensor") // 2, image // 2, image % 2
    block = dy.shape[2]
    features = acts.shape[3]
    heads, head_size = w_qkv.shape[2], w_qkv.shape[4]
    gains = norm_gain[0]
    score_scale = 1.0 / math.sqrt(head_size)
    first = core == 0

    dy_own = send(dy[0, 0], SWAP)

    shared = lax.all_to_all(
        jnp.broadcast_to(perturb, (32, *perturb.shape)), ("member", "image"), 0, 0
    ).reshape(-1, features)

    w_back = w_out[0].reshape(heads * head_size, features)
    w_mat = w_qkv[0].reshape(features, heads * 3 * head_size).T
    split = w_mat.shape[0] // 8
    split_back = w_back.shape[0] // 8
    mine = jnp.concatenate(
        [
            lax.dynamic_slice_in_dim(w_back, image * split_back, split_back, 0),
            lax.dynamic_slice_in_dim(w_mat, image * split, split, 0),
        ],
        axis=0,
    )
    half = mine.shape[0] // 2
    parts = [send(mine[:half], ZL), send(mine[half:], ZL)]

    dy_left, dy_right, dy_far = ring_blocks(dy_own)
    inputs = after(acts[0, 0], dy_own).astype(F32) + shared.astype(F32)
    inputs = inputs.astype(BF)
    in_own = after(send(inputs, SWAP), dy_left)
    in_left, in_right, in_far = ring_blocks(in_own)
    dy_far = [after(piece, in_own) for piece in dy_far]
    rows_dy = placed([dy_own, dy_left, dy_right, jnp.concatenate(dy_far, axis=0)], own_x)
    rows_in = placed([in_own, in_left, in_right, jnp.concatenate(in_far, axis=0)], own_x)
    spread = spread_of(rows_in)
    unit = rows_in.astype(F32) / spread
    normed = (unit * gains).astype(BF)

    def around(part, *seen):
        return exchange(jnp.broadcast_to(after(part, *seen), (4, *part.shape)), "image")

    first_part = around(parts[0], inputs)
    second_part = after(around(parts[1], in_own), in_left)
    pairs = [(part, send(part, CORE)) for part in (first_part, second_part)]

    def joined(pieces):
        mine = jnp.concatenate([piece[0] for piece in pieces], axis=1)
        came = jnp.concatenate([piece[1] for piece in pieces], axis=1)
        both = [jnp.where(first, mine, came), jnp.where(first, came, mine)]
        return jnp.stack(both, axis=1).reshape(-1, features)

    w_back_other = joined([[piece[:, :split_back] for piece in pairs[0]]])
    w_mat_other = joined([[piece[:, split_back:] for piece in pairs[0]], pairs[1]])

    up = matmul_t(rows_dy, w_back).astype(BF)
    packed = matmul_t(normed, w_mat).astype(BF)
    up_other = matmul_t(rows_dy, w_back_other).astype(BF)
    packed_other = matmul_t(normed, w_mat_other).astype(BF)
    both = jnp.concatenate([packed, up], axis=1)
    both_other = jnp.concatenate([packed_other, up_other], axis=1)
    keep = jnp.where(first, both, both_other)
    came = send(jnp.where(first, both_other, both), CORE)
    table = jnp.concatenate([keep, came], axis=0)
    pieces = []
    for head in range(heads):
        at = [(head * 3 + slot) * head_size for slot in range(3)] + [
            (heads * 3 + head) * head_size
        ]
        query, keys, values, upstream = [table[:, a : a + head_size] for a in at]
        pieces.extend(head_grads(query, keys, values, upstream, score_scale))
    grads = jnp.concatenate(pieces, axis=1)
    count = grads.shape[0] // 2
    mine, came = grads[:count], send(grads[count:], CORE)
    grads_own = jnp.where(first, mine, came)
    grads_other = jnp.where(first, came, mine)

    along = [
        jnp.sum(grad.astype(F32) * value.astype(F32), axis=-1, keepdims=True)
        for grad, value in ((grads_own, packed), (grads_other, packed_other))
    ]
    centre = (along[0] + along[1]) / features

    def partial(values, weight):
        part = lax.dot_general(
            values, weight, (((1,), (0,)), ((), ())), preferred_element_type=F32
        )
        return lax.optimization_barrier(part.astype(BF)).astype(F32)

    def result_of(start, stop, *seen):
        part = slice(start, stop)
        grad = partial(after(grads_own, *seen), w_mat[:, part])
        grad = grad + partial(after(grads_other, *seen), w_mat_other[:, part])
        value = (gains[part] * grad - unit[:, part] * centre) / spread
        value = value.reshape(4, block, stop - start) + jnp.where(
            lax.iota(jnp.int32, 4)[:, None, None] == own_x, dy_own[:, part].astype(F32), 0.0
        )
        return value.astype(BF).reshape(4, 4, 4, 8, stop - start)

    cut = 1920

    def summed(value, axis):
        return jnp.sum(exchange(value, axis).astype(F32), axis=0)

    def over_y(value, dim):
        total = lax.dynamic_index_in_dim(value, own_y, dim, keepdims=False).astype(F32)
        for step in (2, 1, -1):
            piece = lax.dynamic_index_in_dim(value, (own_y + step) % 4, dim, keepdims=False)
            total = total + send(piece, Y[step]).astype(F32)
        return total

    result_a = result_of(0, cut)
    result_b = result_of(cut, features, result_a)
    part_a = summed(result_a, "tensor")
    part_b = over_y(result_b, 2)
    part_a = over_y(part_a.astype(BF), 1)
    part_b = summed(part_b.astype(BF), "tensor")
    total = jnp.concatenate([part_a, part_b], axis=-1)
    total = summed(total, "member")
    total = send(total, SWAP).reshape(2, 4, features)
    low, high = total[0], total[1]
    return jnp.where(first, low, high) + send(jnp.where(first, high, low), CORE)


def solution(mesh):
    in_specs = (
        P("member", "image", "tensor", None),
        P(("tensor", "member", "image"), None),
        P("member", "image", "tensor", None),
        P("member", None),
        P("member", None, "tensor", None, None),
        P("member", "tensor", None, None),
    )
    out_specs = P(("tensor", "member", "image"), None)
    return jax.shard_map(
        on_device, mesh=mesh, in_specs=in_specs, out_specs=out_specs, check_vma=False
    )
```

```python
import math

import jax
import jax.numpy as jnp
from jax import lax
from jax.experimental import pallas as pl
from jax.experimental.pallas import tpu as pltpu
from jax.sharding import PartitionSpec as P

AXES = ("tensor", "member", "image")
BF = jnp.bfloat16
F32 = jnp.float32


def routes(move):
    pairs = []
    for x in range(4):
        for zl in range(2):
            for zh in range(4):
                for y in range(4):
                    for c in range(2):
                        nx, nzl, nzh, ny, nc = move(x, zl, zh, y, c)
                        pairs.append(
                            (
                                ((x * 2 + zl) * 4 + zh) * 8 + y * 2 + c,
                                (((nx % 4) * 2 + nzl) * 4 + nzh % 4) * 8 + (ny % 4) * 2 + nc,
                            )
                        )
    return [(source, target) for source, target in pairs if source != target]


SWAP = routes(lambda x, zl, zh, y, c: (x, c, zh, y, zl))
CORE = routes(lambda x, zl, zh, y, c: (x, zl, zh, y, 1 - c))
ZL = routes(lambda x, zl, zh, y, c: (x, 1 - zl, zh, y, c))
X = {d: routes(lambda x, zl, zh, y, c, d=d: (x + d, zl, zh, y, c)) for d in (-1, 1, 2)}

Y = {d: routes(lambda x, zl, zh, y, c, d=d: (x, zl, zh, y + d, c)) for d in (-1, 1, 2)}
Z = {d: routes(lambda x, zl, zh, y, c, d=d: (x, zl, zh + d, y, c)) for d in (-1, 1, 2)}


BLOCKS = [
    [
        ((x * 2 + zl) * 4 + zh) * 8 + y * 2 + c
        for zl in range(2)
        for zh in range(4)
        for y in range(4)
    ]
    for x in range(4)
    for c in range(2)
]


def send(value, pairs):
    return lax.ppermute(value, AXES, pairs)


def together(*values):
    return lax.optimization_barrier(values)


def swapped(value, stays):
    return jnp.where(stays, value, send(value, SWAP))


def rows_of_weights(raw, scratch, rows):
    scratch[...] = raw.astype(F32)
    return [scratch[pl.ds(column, rows, stride=6), :].astype(BF) for column in range(6)]


def own_weights_body(raw_ref, out_ref, scratch):
    rows = out_ref.shape[0]
    for column, value in enumerate(rows_of_weights(raw_ref[...], scratch, rows)):
        out_ref[:, column * 128 : (column + 1) * 128] = value


def own_weights(raw):
    count, step = raw.shape[0] // 6, 400
    return pl.pallas_call(
        own_weights_body,
        grid=(count // step,),
        in_specs=[pl.BlockSpec((step * 6, 128), lambda i: (i, 0))],
        out_specs=pl.BlockSpec((step, 768), lambda i: (i, 0)),
        out_shape=jax.ShapeDtypeStruct((count, 768), BF),
        scratch_shapes=[pltpu.VMEM((step * 6, 128), F32)],
        compiler_params=pltpu.CompilerParams(vmem_limit_bytes=16 << 20),
        cost_estimate=pl.CostEstimate(flops=0, bytes_accessed=40 << 20, transcendentals=0),
        name="own_weights",
    )(raw)


def other_weights_body(place_ref, p0, p1, p2, p3, mat_ref, back_ref, scratch, scratch_back):
    for ref, step in ((p0, 0), (p1, 3), (p2, 1), (p3, 2)):
        place = (place_ref[0] + step) % 4
        at = pl.multiple_of(place * 400, 16)
        for column, value in enumerate(rows_of_weights(ref[:2400, :], scratch, 400)):
            mat_ref[pl.ds(at, 400), column * 128 : (column + 1) * 128] = value
        scratch_back[...] = ref[2400:, :].astype(F32)
        for pair in range(2):
            row = pl.multiple_of(place * 32 + pair * 16, 16)
            for column in range(25):
                upper = scratch_back[(pair * 50 + column) * 8 : (pair * 50 + column) * 8 + 8, :]
                lower = scratch_back[(pair * 50 + 25 + column) * 8 : (pair * 50 + 25 + column) * 8 + 8, :]
                back_ref[pl.ds(row, 16), column * 128 : (column + 1) * 128] = jnp.concatenate(
                    [upper, lower], axis=0
                ).astype(BF)


def other_weights(pieces, place):
    whole = pl.BlockSpec(memory_space=pltpu.VMEM)
    return pl.pallas_call(
        other_weights_body,
        in_specs=[pl.BlockSpec(memory_space=pltpu.SMEM), whole, whole, whole, whole],
        out_specs=[whole, whole],
        out_shape=[jax.ShapeDtypeStruct((1600, 768), BF), jax.ShapeDtypeStruct((128, 3200), BF)],
        scratch_shapes=[pltpu.VMEM((2400, 128), F32), pltpu.VMEM((800, 128), F32)],
        compiler_params=pltpu.CompilerParams(vmem_limit_bytes=32 << 20),
        cost_estimate=pl.CostEstimate(flops=0, bytes_accessed=40 << 20, transcendentals=0),
        name="other_weights",
    )(place.reshape(1), *pieces)


def normed_body(own, left, right, far, gains_ref, normed_ref, rows_ref, spread_ref):
    start = 0
    for ref in (own, left, right, far):
        for part in range(ref.shape[0] // 64):
            values = ref[part * 64 : part * 64 + 64, :]
            floats = values.astype(F32)
            spread = jnp.sqrt(jnp.mean(floats * floats, axis=-1, keepdims=True) + 1e-06)
            at = slice(start, start + 64)
            normed_ref[at, :] = (floats / spread * gains_ref[...]).astype(BF)
            rows_ref[at, :] = values
            spread_ref[at, :] = jnp.broadcast_to(spread, (64, 128))
            start += 64


def normed_rows(pieces, gains):
    whole = pl.BlockSpec(memory_space=pltpu.VMEM)
    return pl.pallas_call(
        normed_body,
        in_specs=[whole] * 5,
        out_specs=[whole] * 3,
        out_shape=[
            jax.ShapeDtypeStruct((512, 3200), BF),
            jax.ShapeDtypeStruct((512, 3200), BF),
            jax.ShapeDtypeStruct((512, 128), F32),
        ],
        compiler_params=pltpu.CompilerParams(vmem_limit_bytes=40 << 20),
        cost_estimate=pl.CostEstimate(flops=0, bytes_accessed=40 << 20, transcendentals=0),
        name="normed_rows",
    )(*pieces, gains)


def result_body(g_own, g_other, w_own, w_other, rows, spread, centre, gains, own_dy, out):
    def partial(grads, weights):
        part = lax.dot_general(
            grads[...], weights[...], (((1,), (1,)), ((), ())), preferred_element_type=F32
        )
        return part.astype(BF).astype(F32)

    grad = partial(g_own, w_own) + partial(g_other, w_other)
    inverse = 1.0 / spread[:, :1]
    along = centre[:, :1] * inverse
    value = (gains[...] * grad - rows[...].astype(F32) * along) * inverse
    count = own_dy.shape[0]
    out[:count, :] = (value[:count] + own_dy[...].astype(F32)).astype(BF)
    out[count:, :] = value[count:].astype(BF)


def result_part(grads, weights, rows, spread, centre, gains, own_dy, start, stop):
    tile = 640
    first = start // tile
    count = rows.shape[0]
    whole = pl.BlockSpec(memory_space=pltpu.VMEM)
    weight = pl.BlockSpec((tile, 768), lambda i: (i + first, 0))
    return pl.pallas_call(
        result_body,
        grid=((stop - start) // tile,),
        in_specs=[
            whole,
            whole,
            weight,
            weight,
            pl.BlockSpec((count, tile), lambda i: (0, i + first)),
            whole,
            whole,
            pl.BlockSpec((1, tile), lambda i: (0, i + first)),
            pl.BlockSpec((own_dy.shape[0], tile), lambda i: (0, i + first)),
        ],
        out_specs=pl.BlockSpec((count, tile), lambda i: (0, i)),
        out_shape=jax.ShapeDtypeStruct((count, stop - start), BF),
        compiler_params=pltpu.CompilerParams(vmem_limit_bytes=40 << 20),
        cost_estimate=pl.CostEstimate(
            flops=4 * count * 768 * (stop - start), bytes_accessed=30 << 20, transcendentals=0
        ),
        name="result_part",
    )(*grads, *weights, rows, spread, centre, gains, own_dy)


def head_grads(query, keys, values, upstream, score_scale):
    scores = jnp.einsum("qe,ke->qk", query, keys, preferred_element_type=F32) * score_scale
    peak = jnp.max(scores, axis=-1, keepdims=True)
    expo = jnp.exp(scores - peak)
    attention = expo / jnp.sum(expo, axis=-1, keepdims=True)
    rounded = attention.astype(BF)
    through = jnp.einsum("qe,ke->qk", upstream, values, preferred_element_type=F32)
    value_grad = jnp.einsum("qk,qe->ke", rounded, upstream, preferred_element_type=F32).astype(BF)
    centre = jnp.sum(attention * through, axis=-1, keepdims=True)
    score_grad = (attention * (through - centre) * score_scale).astype(BF)
    query_grad = jnp.einsum("qk,ke->qe", score_grad, keys, preferred_element_type=F32).astype(BF)
    key_grad = jnp.einsum("qk,qe->ke", score_grad, query, preferred_element_type=F32).astype(BF)
    return (query_grad, key_grad, value_grad)


def matmul(left, right, dims):
    return lax.dot_general(left, right, ((dims[:1], dims[1:]), ((), ())), preferred_element_type=F32)


def on_device(acts, perturb, dy, norm_gain, w_qkv, w_out):
    tensor, member, image = [lax.axis_index(axis) for axis in AXES]
    own_y, core = image // 2, image % 2
    first, stays = core == 0, core == tensor % 2
    features = acts.shape[3]
    heads, head_size = w_qkv.shape[2], w_qkv.shape[4]
    score_scale = 1.0 / math.sqrt(head_size)

    dy_own = swapped(dy[0, 0], stays)
    own_acts = swapped(acts[0, 0], stays)

    raw = w_qkv[0].transpose(0, 2, 1, 3).reshape(-1, head_size)
    w_back = w_out[0].reshape(heads * head_size, features)
    tiles = w_back.reshape(-1, 8, features // 128, 128).transpose(0, 2, 1, 3).reshape(-1, 128)
    eighth = core * 4 + own_y
    piece = jnp.concatenate(
        [
            lax.dynamic_slice_in_dim(array, eighth * (array.shape[0] // 8), array.shape[0] // 8, 0)
            for array in (raw, tiles)
        ],
        axis=0,
    )
    piece_other = send(piece, ZL)

    few = swapped(perturb, stays)
    shared = lax.all_to_all(
        jnp.broadcast_to(few, (32, *few.shape)), AXES, 0, 0, axis_index_groups=BLOCKS
    )
    shared = shared.reshape(2, 4, 4, *few.shape).transpose(1, 2, 0, 3, 4).reshape(-1, features)

    dy_left, dy_right, dy_far = [send(dy_own, X[step]) for step in (1, -1, 2)]
    pieces = [piece_other] + [send(piece_other, Y[step]) for step in (1, -1, 2)]
    shared, dy_left, dy_right = together(shared, dy_left, dy_right)
    in_own = (own_acts.astype(F32) + shared.astype(F32)).astype(BF)
    in_own, raw = together(in_own, raw)
    w_mat = own_weights(raw)
    in_left, in_right, in_far = [send(in_own, X[step]) for step in (1, -1, 2)]
    mat_half, back_half = other_weights(pieces, own_y)

    def joined(mine):
        came = send(mine, CORE)
        return jnp.concatenate(
            [jnp.where(first, mine, came), jnp.where(first, came, mine)], axis=0
        )

    w_back_other, w_mat_other = joined(back_half), joined(mat_half)

    rows_dy = jnp.concatenate([dy_own, dy_left, dy_right, dy_far], axis=0)
    normed, rows_in, spread = normed_rows([in_own, in_left, in_right, in_far], norm_gain)
    up = matmul(rows_dy, w_back, (1, 1)).astype(BF)
    packed = matmul(normed, w_mat, (1, 0)).astype(BF)
    up_other = matmul(rows_dy, w_back_other, (1, 1)).astype(BF)
    packed_other = matmul(normed, w_mat_other, (1, 0)).astype(BF)
    both = jnp.concatenate([packed, up], axis=1)
    both_other = jnp.concatenate([packed_other, up_other], axis=1)
    keep = jnp.where(first, both, both_other)
    came = send(jnp.where(first, both_other, both), CORE)
    table = jnp.concatenate([keep, came], axis=0)
    pieces = []
    for head in range(heads):
        at = [(slot * heads + head) * head_size for slot in range(4)]
        query, keys, values, upstream = [table[:, a : a + head_size] for a in at]
        pieces.append(head_grads(query, keys, values, upstream, score_scale))
    grads = jnp.concatenate([piece[slot] for slot in range(3) for piece in pieces], axis=1)
    count = grads.shape[0] // 2
    mine, came = grads[:count], send(grads[count:], CORE)
    grads_own = jnp.where(first, mine, came)
    grads_other = jnp.where(first, came, mine)

    along = [
        jnp.sum(grad.astype(F32) * value.astype(F32), axis=-1, keepdims=True)
        for grad, value in ((grads_own, packed), (grads_other, packed_other))
    ]
    centre = jnp.broadcast_to((along[0] + along[1]) / features, spread.shape)

    def result_of(grads, start, stop):
        return result_part(
            grads,
            [w_mat, w_mat_other],
            rows_in,
            spread,
            centre,
            norm_gain,
            dy_own,
            start,
            stop,
        )

    def over_x(value):
        count = value.shape[0] // 4
        total = value[:count].astype(F32)
        for place, step in ((3, 2), (1, -1), (2, 1)):
            piece = value[place * count : (place + 1) * count]
            total = total + send(piece, X[step]).astype(F32)
        return total.astype(BF)

    def over(value, ring, own, dim):
        total = lax.dynamic_index_in_dim(value, own, dim, keepdims=False).astype(F32)
        for step in (2, 1, -1):
            piece = lax.dynamic_index_in_dim(value, (own + step) % 4, dim, keepdims=False)
            total = total + send(piece, ring[step]).astype(F32)
        return total

    cut = 1920
    result_a = result_of([grads_own, grads_other], 0, cut)
    result_a, grads_own, grads_other = together(result_a, grads_own, grads_other)
    result_b = result_of([grads_own, grads_other], cut, features)
    part_a = together(over_x(result_a))[0]
    part_b = over(result_b.reshape(4, 4, 4, 8, -1), Y, own_y, 2).astype(BF)
    part_a = over(part_a.reshape(4, 4, 8, -1), Y, own_y, 1)
    part_b = over_x(part_b.reshape(128, -1)).reshape(4, 8, -1)
    total = jnp.concatenate([part_a.astype(BF), part_b], axis=-1)
    total = over(total, Z, member, 0)
    total = swapped(total, stays).reshape(2, 4, features)
    low, high = total[0], total[1]
    return jnp.where(first, low, high) + send(jnp.where(first, high, low), CORE)


def solution(mesh):
    in_specs = (
        P("member", "image", "tensor", None),
        P(("tensor", "member", "image"), None),
        P("member", "image", "tensor", None),
        P("member", None),
        P("member", None, "tensor", None, None),
        P("member", "tensor", None, None),
    )
    out_specs = P(("tensor", "member", "image"), None)
    return jax.shard_map(
        on_device, mesh=mesh, in_specs=in_specs, out_specs=out_specs, check_vma=False
    )
```

```python
import functools
import math

import jax
import jax.numpy as jnp
from jax import lax
from jax.experimental import pallas as pl
from jax.experimental.pallas import tpu as pltpu
from jax.sharding import PartitionSpec as P

AXES = ("tensor", "member", "image")
BF = jnp.bfloat16
F32 = jnp.float32


def routes(move):
    pairs = []
    for x in range(4):
        for zl in range(2):
            for zh in range(4):
                for y in range(4):
                    for c in range(2):
                        nx, nzl, nzh, ny, nc = move(x, zl, zh, y, c)
                        pairs.append(
                            (
                                ((x * 2 + zl) * 4 + zh) * 8 + y * 2 + c,
                                (((nx % 4) * 2 + nzl) * 4 + nzh % 4) * 8 + (ny % 4) * 2 + nc,
                            )
                        )
    return [(source, target) for source, target in pairs if source != target]


SWAP = routes(lambda x, zl, zh, y, c: (x, c, zh, y, zl))
CORE = routes(lambda x, zl, zh, y, c: (x, zl, zh, y, 1 - c))
ZL = routes(lambda x, zl, zh, y, c: (x, 1 - zl, zh, y, c))
X = {d: routes(lambda x, zl, zh, y, c, d=d: (x + d, zl, zh, y, c)) for d in (-1, 1, 2)}

Y = {d: routes(lambda x, zl, zh, y, c, d=d: (x, zl, zh, y + d, c)) for d in (-1, 1, 2)}
Z = {d: routes(lambda x, zl, zh, y, c, d=d: (x, zl, zh + d, y, c)) for d in (-1, 1, 2)}


BLOCKS = [
    [(t * 4 + zh) * 8 + y * 2 + c for zh in range(4) for y in range(4)]
    for t in range(8)
    for c in range(2)
]


def send(value, pairs):
    return lax.ppermute(value, AXES, pairs)


def together(*values):
    return lax.optimization_barrier(values)


def swapped(value, stays):
    return jnp.where(stays, value, send(value, SWAP))


def rows_of_weights(raw, scratch, rows):
    scratch[...] = raw.astype(F32)
    return [scratch[pl.ds(column, rows, stride=6), :].astype(BF) for column in range(6)]


def own_weights_body(raw_ref, out_ref, scratch):
    rows = out_ref.shape[0]
    for column, value in enumerate(rows_of_weights(raw_ref[...], scratch, rows)):
        out_ref[:, column * 128 : (column + 1) * 128] = value


def own_weights(raw):
    count, step = raw.shape[0] // 6, 400
    return pl.pallas_call(
        own_weights_body,
        grid=(count // step,),
        in_specs=[pl.BlockSpec((step * 6, 128), lambda i: (i, 0))],
        out_specs=pl.BlockSpec((step, 768), lambda i: (i, 0)),
        out_shape=jax.ShapeDtypeStruct((count, 768), BF),
        scratch_shapes=[pltpu.VMEM((step * 6, 128), F32)],
        compiler_params=pltpu.CompilerParams(vmem_limit_bytes=16 << 20),
        cost_estimate=pl.CostEstimate(flops=0, bytes_accessed=40 << 20, transcendentals=0),
        name="own_weights",
    )(raw)


def other_weights_body(place_ref, p0, p1, p2, p3, mat_ref, back_ref, scratch, scratch_back):
    for ref, step in ((p0, 0), (p1, 3), (p2, 1), (p3, 2)):
        place = (place_ref[0] + step) % 4
        at = pl.multiple_of(place * 400, 16)
        for column, value in enumerate(rows_of_weights(ref[:2400, :], scratch, 400)):
            mat_ref[pl.ds(at, 400), column * 128 : (column + 1) * 128] = value
        scratch_back[...] = ref[2400:, :].astype(F32)
        for pair in range(2):
            row = pl.multiple_of(place * 32 + pair * 16, 16)
            for column in range(25):
                upper = scratch_back[(pair * 50 + column) * 8 : (pair * 50 + column) * 8 + 8, :]
                lower = scratch_back[(pair * 50 + 25 + column) * 8 : (pair * 50 + 25 + column) * 8 + 8, :]
                back_ref[pl.ds(row, 16), column * 128 : (column + 1) * 128] = jnp.concatenate(
                    [upper, lower], axis=0
                ).astype(BF)


def other_weights(pieces, place):
    whole = pl.BlockSpec(memory_space=pltpu.VMEM)
    return pl.pallas_call(
        other_weights_body,
        in_specs=[pl.BlockSpec(memory_space=pltpu.SMEM), whole, whole, whole, whole],
        out_specs=[whole, whole],
        out_shape=[jax.ShapeDtypeStruct((1600, 768), BF), jax.ShapeDtypeStruct((128, 3200), BF)],
        scratch_shapes=[pltpu.VMEM((2400, 128), F32), pltpu.VMEM((800, 128), F32)],
        compiler_params=pltpu.CompilerParams(vmem_limit_bytes=32 << 20),
        cost_estimate=pl.CostEstimate(flops=0, bytes_accessed=40 << 20, transcendentals=0),
        name="other_weights",
    )(place.reshape(1), *pieces)


def normed_body(own, left, right, far, gains_ref, normed_ref, rows_ref, spread_ref):
    start = 0
    for ref in (own, left, right, far):
        for part in range(ref.shape[0] // 64):
            values = ref[part * 64 : part * 64 + 64, :]
            floats = values.astype(F32)
            spread = jnp.sqrt(jnp.mean(floats * floats, axis=-1, keepdims=True) + 1e-06)
            at = slice(start, start + 64)
            normed_ref[at, :] = (floats / spread * gains_ref[...]).astype(BF)
            rows_ref[at, :] = values
            spread_ref[at, :] = jnp.broadcast_to(spread, (64, 128))
            start += 64


def normed_rows(pieces, gains):
    whole = pl.BlockSpec(memory_space=pltpu.VMEM)
    return pl.pallas_call(
        normed_body,
        in_specs=[whole] * 5,
        out_specs=[whole] * 3,
        out_shape=[
            jax.ShapeDtypeStruct((512, 3200), BF),
            jax.ShapeDtypeStruct((512, 3200), BF),
            jax.ShapeDtypeStruct((512, 128), F32),
        ],
        compiler_params=pltpu.CompilerParams(vmem_limit_bytes=40 << 20),
        cost_estimate=pl.CostEstimate(flops=0, bytes_accessed=40 << 20, transcendentals=0),
        name="normed_rows",
    )(*pieces, gains)


def result_body(start, g_own, g_other, p_own, p_other, w_own, w_low, w_high, rows, spread, gains, own_dy, out):
    along = 0.0
    for grads, values in ((g_own, p_own), (g_other, p_other)):
        along = along + jnp.sum(
            grads[...].astype(F32) * values[...].astype(F32), axis=-1, keepdims=True
        )
    inverse = 1.0 / spread[:, :1]
    along = along * (inverse / w_own.shape[0])
    count, middle = own_dy.shape[0], w_low.shape[0]
    tile = 256
    for at in range(start, start + out.shape[1], tile):
        end = min(at + tile, start + out.shape[1])
        weights = []
        if at < middle:
            weights.append(w_low[at : min(end, middle), :])
        if end > middle:
            weights.append(w_high[max(at, middle) - middle : end - middle, :])
        weights = jnp.concatenate(weights, axis=0) if len(weights) > 1 else weights[0]
        own = matmul(g_own[...], w_own[at:end, :], (1, 1)).astype(BF).astype(F32)
        grad = own + matmul(g_other[...], weights, (1, 1)).astype(BF).astype(F32)
        value = (gains[:, at:end] * grad - rows[:, at:end].astype(F32) * along) * inverse
        to = slice(at - start, end - start)
        out[:count, to] = (value[:count] + own_dy[:, at:end].astype(F32)).astype(BF)
        out[count:, to] = value[count:].astype(BF)


def result_part(arrays, start, stop):
    count = arrays[0].shape[0]
    whole = pl.BlockSpec(memory_space=pltpu.VMEM)
    return pl.pallas_call(
        functools.partial(result_body, start),
        in_specs=[whole] * len(arrays),
        out_specs=whole,
        out_shape=jax.ShapeDtypeStruct((count, stop - start), BF),
        compiler_params=pltpu.CompilerParams(vmem_limit_bytes=48 << 20),
        name="result_part",
    )(*arrays)


def attention_body(keep_ref, came_ref, mine_ref, theirs_ref, table, grads, key_sum, value_sum):
    half = keep_ref.shape[0]
    rows = 2 * half
    step = 256
    scale = 1.0 / math.sqrt(128)
    table[:half, :] = keep_ref[...]
    table[half:, :] = came_ref[...]
    for head in range(2):
        at = [(slot * 2 + head) * 128 for slot in range(4)]
        query_at, key_at, value_at, up_at = [slice(a, a + 128) for a in at]
        keys_t = table[:, key_at].astype(F32).T.astype(BF)

        def block(index, carry, query_at=query_at, key_at=key_at, value_at=value_at, up_at=up_at, keys_t=keys_t):
            here = pl.ds(pl.multiple_of(index * step, step), step)
            query, upstream = table[here, query_at], table[here, up_at]
            scores = matmul(table[:, key_at], query, (1, 1))
            peak = jnp.max(scores, axis=0, keepdims=True)
            expo = jnp.exp((scores - peak) * scale)
            attention = expo * (1.0 / jnp.sum(expo, axis=0, keepdims=True))
            through = matmul(table[:, value_at], upstream, (1, 1))
            value_part = matmul(attention.astype(BF), upstream, (1, 0))
            centre = jnp.sum(attention * through, axis=0, keepdims=True)
            score_grad = (attention * (through - centre) * scale).astype(BF)
            key_part = matmul(score_grad, query, (1, 0))
            grads[here, query_at] = matmul(keys_t, score_grad, (1, 0)).T.astype(BF)

            @pl.when(index == 0)
            def _():
                key_sum[...] = key_part
                value_sum[...] = value_part

            @pl.when(index > 0)
            def _():
                key_sum[...] += key_part
                value_sum[...] += value_part

            return carry

        lax.fori_loop(0, rows // step, block, 0)
        grads[:, key_at] = key_sum[...].astype(BF)
        grads[:, value_at] = value_sum[...].astype(BF)
    mine_ref[...] = grads[:half, :]
    theirs_ref[...] = grads[half:, :]


def attention_grads(keep, came):
    half = keep.shape[0]
    whole = pl.BlockSpec(memory_space=pltpu.VMEM)
    return pl.pallas_call(
        attention_body,
        in_specs=[whole, whole],
        out_specs=[whole, whole],
        out_shape=[jax.ShapeDtypeStruct((half, 768), BF)] * 2,
        scratch_shapes=[
            pltpu.VMEM((2 * half, 1024), BF),
            pltpu.VMEM((2 * half, 768), BF),
            pltpu.VMEM((2 * half, 128), F32),
            pltpu.VMEM((2 * half, 128), F32),
        ],
        compiler_params=pltpu.CompilerParams(vmem_limit_bytes=40 << 20),
        name="attention_grads",
    )(keep, came)


def matmul(left, right, dims):
    return lax.dot_general(left, right, ((dims[:1], dims[1:]), ((), ())), preferred_element_type=F32)


def on_device(acts, perturb, dy, norm_gain, w_qkv, w_out):
    tensor, member, image = [lax.axis_index(axis) for axis in AXES]
    own_y, core = image // 2, image % 2
    first, stays = core == 0, core == tensor % 2
    features = acts.shape[3]
    heads, head_size = w_qkv.shape[2], w_qkv.shape[4]

    dy_own = swapped(dy[0, 0], stays)

    rows = lax.all_to_all(
        jnp.broadcast_to(perturb, (16, *perturb.shape)), AXES, 0, 0, axis_index_groups=BLOCKS
    )
    rows, dy_own = together(rows, dy_own)
    other = send(rows, CORE)
    shared = jnp.stack([jnp.where(first, rows, other), jnp.where(first, other, rows)], axis=1)
    inputs = acts[0, 0].astype(F32) + shared.reshape(-1, features).astype(F32)
    inputs = inputs.astype(BF)

    raw = w_qkv[0].transpose(0, 2, 1, 3).reshape(-1, head_size)
    w_back = w_out[0].reshape(heads * head_size, features)
    tiles = w_back.reshape(-1, 8, features // 128, 128).transpose(0, 2, 1, 3).reshape(-1, 128)
    eighth = core * 4 + own_y
    piece = jnp.concatenate(
        [
            lax.dynamic_slice_in_dim(array, eighth * (array.shape[0] // 8), array.shape[0] // 8, 0)
            for array in (raw, tiles)
        ],
        axis=0,
    )
    piece, dy_own = together(piece, dy_own)
    piece_other = send(piece, ZL)

    dy_left, dy_right, dy_far = [send(dy_own, X[step]) for step in (1, -1, 2)]
    pieces = [piece_other] + [send(piece_other, Y[step]) for step in (1, -1, 2)]
    in_own = swapped(inputs, stays)
    in_own, raw = together(in_own, raw)
    w_mat = own_weights(raw)
    in_left, in_right, in_far = [send(in_own, X[step]) for step in (1, -1, 2)]
    mat_half, back_half = other_weights(pieces, own_y)

    def joined(mine):
        came = send(mine, CORE)
        return jnp.where(first, mine, came), jnp.where(first, came, mine)

    w_back_other = jnp.concatenate(joined(back_half), axis=0)
    w_low, w_high = joined(mat_half)

    rows_dy = jnp.concatenate([dy_own, dy_left, dy_right, dy_far], axis=0)
    normed, rows_in, spread = normed_rows([in_own, in_left, in_right, in_far], norm_gain)
    up = matmul(rows_dy, w_back, (1, 1)).astype(BF)
    packed = matmul(normed, w_mat, (1, 0)).astype(BF)
    up_other = matmul(rows_dy, w_back_other, (1, 1)).astype(BF)
    packed_other = matmul(normed, jnp.concatenate([w_low, w_high], axis=0), (1, 0)).astype(BF)
    both = jnp.concatenate([packed, up], axis=1)
    both_other = jnp.concatenate([packed_other, up_other], axis=1)
    keep = jnp.where(first, both, both_other)
    came = send(jnp.where(first, both_other, both), CORE)
    mine, theirs = attention_grads(keep, came)
    came = send(theirs, CORE)
    grads_own = jnp.where(first, mine, came)
    grads_other = jnp.where(first, came, mine)

    def result_of(grads, start, stop):
        arrays = [*grads, packed, packed_other, w_mat, w_low, w_high, rows_in, spread, norm_gain]
        return result_part([*arrays, dy_own], start, stop)

    def over_x(value):
        count = value.shape[0] // 4
        total = value[:count].astype(F32)
        for place, step in ((3, 2), (1, -1), (2, 1)):
            piece = value[place * count : (place + 1) * count]
            total = total + send(piece, X[step]).astype(F32)
        return total.astype(BF)

    def over(value, ring, own, dim):
        total = lax.dynamic_index_in_dim(value, own, dim, keepdims=False).astype(F32)
        for step in (2, 1, -1):
            piece = lax.dynamic_index_in_dim(value, (own + step) % 4, dim, keepdims=False)
            total = total + send(piece, ring[step]).astype(F32)
        return total

    cut = 1664
    result_a = result_of([grads_own, grads_other], 0, cut)
    result_a, grads_own, grads_other = together(result_a, grads_own, grads_other)
    result_b = result_of([grads_own, grads_other], cut, features)
    part_a = together(over_x(result_a))[0]
    part_b = over(result_b.reshape(4, 4, 4, 8, -1), Y, own_y, 2).astype(BF)
    part_a = over(part_a.reshape(4, 4, 8, -1), Y, own_y, 1)
    part_b = over_x(part_b.reshape(128, -1)).reshape(4, 8, -1)
    total = jnp.concatenate([part_a.astype(BF), part_b], axis=-1)
    total = over(total, Z, member, 0)
    total = swapped(total, stays).reshape(2, 4, features)
    low, high = total[0], total[1]
    return jnp.where(first, low, high) + send(jnp.where(first, high, low), CORE)


def solution(mesh):
    in_specs = (
        P("member", "image", "tensor", None),
        P(("tensor", "member", "image"), None),
        P("member", "image", "tensor", None),
        P("member", None),
        P("member", None, "tensor", None, None),
        P("member", "tensor", None, None),
    )
    out_specs = P(("tensor", "member", "image"), None)
    return jax.shard_map(
        on_device, mesh=mesh, in_specs=in_specs, out_specs=out_specs, check_vma=False
    )
```

```python
import functools
import math

import jax
import jax.numpy as jnp
from jax import lax
from jax.experimental import pallas as pl
from jax.experimental.pallas import tpu as pltpu
from jax.sharding import PartitionSpec as P

AXES = ("tensor", "member", "image")
BF = jnp.bfloat16
F32 = jnp.float32


def routes(move):
    pairs = []
    for x in range(4):
        for zl in range(2):
            for zh in range(4):
                for y in range(4):
                    for c in range(2):
                        nx, nzl, nzh, ny, nc = move(x, zl, zh, y, c)
                        pairs.append(
                            (
                                ((x * 2 + zl) * 4 + zh) * 8 + y * 2 + c,
                                (((nx % 4) * 2 + nzl) * 4 + nzh % 4) * 8 + (ny % 4) * 2 + nc,
                            )
                        )
    return [(source, target) for source, target in pairs if source != target]


SWAP = routes(lambda x, zl, zh, y, c: (x, c, zh, y, zl))
TURN = routes(lambda x, zl, zh, y, c: (x, c, zh, y, 1 - zl))
CORE = routes(lambda x, zl, zh, y, c: (x, zl, zh, y, 1 - c))
ZL = routes(lambda x, zl, zh, y, c: (x, 1 - zl, zh, y, c))
X = {d: routes(lambda x, zl, zh, y, c, d=d: (x + d, zl, zh, y, c)) for d in (-1, 1, 2)}

Y = {d: routes(lambda x, zl, zh, y, c, d=d: (x, zl, zh, y + d, c)) for d in (-1, 1, 2)}
Z = {d: routes(lambda x, zl, zh, y, c, d=d: (x, zl, zh + d, y, c)) for d in (-1, 1, 2)}


BLOCKS = [
    [(t * 4 + zh) * 8 + y * 2 + c for zh in range(4) for y in range(4)]
    for t in range(8)
    for c in range(2)
]


def send(value, pairs):
    return lax.ppermute(value, AXES, pairs)


def together(*values):
    return lax.optimization_barrier(values)


def swapped(value, stays):
    return jnp.where(stays, value, send(value, SWAP))


def rows_of_weights(raw, scratch, rows):
    scratch[...] = raw.astype(F32)
    return [scratch[pl.ds(column, rows, stride=6), :].astype(BF) for column in range(6)]


def own_weights_body(raw_ref, out_ref, scratch):
    rows = out_ref.shape[0]
    for column, value in enumerate(rows_of_weights(raw_ref[...], scratch, rows)):
        out_ref[:, column * 128 : (column + 1) * 128] = value


def own_weights(raw):
    count, step = raw.shape[0] // 6, 400
    return pl.pallas_call(
        own_weights_body,
        grid=(count // step,),
        in_specs=[pl.BlockSpec((step * 6, 128), lambda i: (i, 0))],
        out_specs=pl.BlockSpec((step, 768), lambda i: (i, 0)),
        out_shape=jax.ShapeDtypeStruct((count, 768), BF),
        scratch_shapes=[pltpu.VMEM((step * 6, 128), F32)],
        compiler_params=pltpu.CompilerParams(vmem_limit_bytes=16 << 20),
        cost_estimate=pl.CostEstimate(flops=0, bytes_accessed=40 << 20, transcendentals=0),
        name="own_weights",
    )(raw)


def other_weights_body(place_ref, p0, p1, p2, p3, mat_ref, back_ref, scratch, scratch_back):
    for ref, step in ((p0, 0), (p1, 3), (p2, 1), (p3, 2)):
        place = (place_ref[0] + step) % 4
        at = pl.multiple_of(place * 400, 16)
        for column, value in enumerate(rows_of_weights(ref[:2400, :], scratch, 400)):
            mat_ref[pl.ds(at, 400), column * 128 : (column + 1) * 128] = value
        scratch_back[...] = ref[2400:, :].astype(F32)
        for pair in range(2):
            row = pl.multiple_of(place * 32 + pair * 16, 16)
            for column in range(25):
                upper = scratch_back[(pair * 50 + column) * 8 : (pair * 50 + column) * 8 + 8, :]
                lower = scratch_back[(pair * 50 + 25 + column) * 8 : (pair * 50 + 25 + column) * 8 + 8, :]
                back_ref[pl.ds(row, 16), column * 128 : (column + 1) * 128] = jnp.concatenate(
                    [upper, lower], axis=0
                ).astype(BF)


def other_weights(pieces, place):
    whole = pl.BlockSpec(memory_space=pltpu.VMEM)
    return pl.pallas_call(
        other_weights_body,
        in_specs=[pl.BlockSpec(memory_space=pltpu.SMEM), whole, whole, whole, whole],
        out_specs=[whole, whole],
        out_shape=[jax.ShapeDtypeStruct((1600, 768), BF), jax.ShapeDtypeStruct((128, 3200), BF)],
        scratch_shapes=[pltpu.VMEM((2400, 128), F32), pltpu.VMEM((800, 128), F32)],
        compiler_params=pltpu.CompilerParams(vmem_limit_bytes=32 << 20),
        cost_estimate=pl.CostEstimate(flops=0, bytes_accessed=40 << 20, transcendentals=0),
        name="other_weights",
    )(place.reshape(1), *pieces)


def normed_body(own, left, right, far_up, far_down, gains_ref, normed_ref, rows_ref, spread_ref):
    start = 0
    for ref in (own, left, right, far_up, far_down):
        for part in range(ref.shape[0] // 64):
            values = ref[part * 64 : part * 64 + 64, :]
            floats = values.astype(F32)
            spread = jnp.sqrt(jnp.mean(floats * floats, axis=-1, keepdims=True) + 1e-06)
            at = slice(start, start + 64)
            normed_ref[at, :] = (floats / spread * gains_ref[...]).astype(BF)
            rows_ref[at, :] = values
            spread_ref[at, :] = jnp.broadcast_to(spread, (64, 128))
            start += 64


def normed_rows(pieces, gains):
    whole = pl.BlockSpec(memory_space=pltpu.VMEM)
    return pl.pallas_call(
        normed_body,
        in_specs=[whole] * 6,
        out_specs=[whole] * 3,
        out_shape=[
            jax.ShapeDtypeStruct((512, 3200), BF),
            jax.ShapeDtypeStruct((512, 3200), BF),
            jax.ShapeDtypeStruct((512, 128), F32),
        ],
        compiler_params=pltpu.CompilerParams(vmem_limit_bytes=40 << 20),
        cost_estimate=pl.CostEstimate(flops=0, bytes_accessed=40 << 20, transcendentals=0),
        name="normed_rows",
    )(*pieces, gains)


def result_body(g_own, g_other, p_own, p_other, w_own, w_other, rows, spread, gains, own_dy, out, along_ref):
    features = 3200

    @pl.when(pl.program_id(0) == 0)
    def _():
        along = 0.0
        for grads, values in ((g_own, p_own), (g_other, p_other)):
            along = along + jnp.sum(
                grads[...].astype(F32) * values[...].astype(F32), axis=-1, keepdims=True
            )
        inverse = 1.0 / spread[...]
        along_ref[0] = inverse
        along_ref[1] = along * inverse * inverse / features

    grad = matmul(g_own[...], w_own[...], (1, 1)).astype(BF).astype(F32)
    grad = grad + matmul(g_other[...], w_other[...], (1, 1)).astype(BF).astype(F32)
    inverse, along = along_ref[0, :, :1], along_ref[1, :, :1]
    value = gains[...] * grad * inverse - rows[...].astype(F32) * along
    count = own_dy.shape[0]
    out[:count, :] = (value[:count] + own_dy[...].astype(F32)).astype(BF)
    out[count:, :] = value[count:].astype(BF)


def result_part(grads, values, weights, rows, spread, gains, own_dy, start, stop):
    tile = 640
    first = start // tile
    count = rows.shape[0]
    whole = pl.BlockSpec(memory_space=pltpu.VMEM)
    weight = pl.BlockSpec((tile, 768), lambda i: (i + first, 0))
    return pl.pallas_call(
        result_body,
        grid=((stop - start) // tile,),
        in_specs=[
            whole,
            whole,
            whole,
            whole,
            weight,
            weight,
            pl.BlockSpec((count, tile), lambda i: (0, i + first)),
            whole,
            pl.BlockSpec((1, tile), lambda i: (0, i + first)),
            pl.BlockSpec((own_dy.shape[0], tile), lambda i: (0, i + first)),
        ],
        out_specs=pl.BlockSpec((count, tile), lambda i: (0, i)),
        out_shape=jax.ShapeDtypeStruct((count, stop - start), BF),
        scratch_shapes=[pltpu.VMEM((2, count, 128), F32)],
        compiler_params=pltpu.CompilerParams(vmem_limit_bytes=40 << 20),
        name="result_part",
    )(*grads, *values, *weights, rows, spread, gains, own_dy)


def joined_body(first_ref, mine, came, out):
    half = mine.shape[0]

    @pl.when(first_ref[0] == 1)
    def _():
        out[:half, :] = mine[...]
        out[half:, :] = came[...]

    @pl.when(first_ref[0] == 0)
    def _():
        out[:half, :] = came[...]
        out[half:, :] = mine[...]


def joined(mine, first):
    whole = pl.BlockSpec(memory_space=pltpu.VMEM)
    return pl.pallas_call(
        joined_body,
        in_specs=[pl.BlockSpec(memory_space=pltpu.SMEM), whole, whole],
        out_specs=whole,
        out_shape=jax.ShapeDtypeStruct((2 * mine.shape[0], mine.shape[1]), BF),
        compiler_params=pltpu.CompilerParams(vmem_limit_bytes=32 << 20),
        name="joined",
    )(first.astype(jnp.int32).reshape(1), mine, send(mine, CORE))


def inputs_body(first_ref, rows, other, acts, out):
    step = rows.shape[1]
    for group in range(0, rows.shape[0], 2):
        parts = []
        for index in (group, group + 1):
            mine, came = rows[index].astype(F32), other[index].astype(F32)
            parts.append(jnp.where(first_ref[0] == 1, mine, came))
            parts.append(jnp.where(first_ref[0] == 1, came, mine))
        at = slice(2 * step * group, 2 * step * (group + 2))
        out[at, :] = (acts[at, :].astype(F32) + jnp.concatenate(parts, axis=0)).astype(BF)


def inputs_of(rows, acts, first):
    whole = pl.BlockSpec(memory_space=pltpu.VMEM)
    return pl.pallas_call(
        inputs_body,
        in_specs=[pl.BlockSpec(memory_space=pltpu.SMEM), whole, whole, whole],
        out_specs=whole,
        out_shape=jax.ShapeDtypeStruct(acts.shape, BF),
        compiler_params=pltpu.CompilerParams(vmem_limit_bytes=16 << 20),
        name="inputs_of",
    )(first.astype(jnp.int32).reshape(1), rows, send(rows, CORE), acts)


def attention_body(keep_ref, came_ref, mine_ref, theirs_ref, table, grads, sums):
    half = keep_ref.shape[0]
    rows = 2 * half
    step = 256
    scale = 1.0 / math.sqrt(128)
    table[:half, :] = keep_ref[...]
    table[half:, :] = came_ref[...]
    heads = range(2)
    slots = [[slice(a, a + 128) for a in ((slot * 2 + head) * 128 for slot in range(4))] for head in heads]
    keys_t = [table[:, slots[head][1]].astype(F32).T.astype(BF) for head in heads]
    sums[...] = jnp.zeros_like(sums)

    def block(index, carry):
        here = pl.ds(pl.multiple_of(index * step, step), step)
        query = [table[here, slots[head][0]] for head in heads]
        upstream = [table[here, slots[head][3]] for head in heads]
        scores = [matmul(table[:, slots[head][1]], query[head], (1, 1)) for head in heads]
        through = [matmul(table[:, slots[head][2]], upstream[head], (1, 1)) for head in heads]
        for head in heads:
            expo = jnp.exp((scores[head] - jnp.max(scores[head], axis=0, keepdims=True)) * scale)
            attention = expo * (1.0 / jnp.sum(expo, axis=0, keepdims=True))
            centre = jnp.sum(attention * through[head], axis=0, keepdims=True)
            score_grad = (attention * (through[head] - centre) * scale).astype(BF)
            sums[2 * head] += matmul(score_grad, query[head], (1, 0))
            sums[2 * head + 1] += matmul(attention.astype(BF), upstream[head], (1, 0))
            grads[here, slots[head][0]] = matmul(keys_t[head], score_grad, (1, 0)).T.astype(BF)
        return carry

    lax.fori_loop(0, rows // step, block, 0)
    for head in heads:
        grads[:, slots[head][1]] = sums[2 * head].astype(BF)
        grads[:, slots[head][2]] = sums[2 * head + 1].astype(BF)
    mine_ref[...] = grads[:half, :]
    theirs_ref[...] = grads[half:, :]


def attention_grads(keep, came):
    half = keep.shape[0]
    whole = pl.BlockSpec(memory_space=pltpu.VMEM)
    return pl.pallas_call(
        attention_body,
        in_specs=[whole, whole],
        out_specs=[whole, whole],
        out_shape=[jax.ShapeDtypeStruct((half, 768), BF)] * 2,
        scratch_shapes=[
            pltpu.VMEM((2 * half, 1024), BF),
            pltpu.VMEM((2 * half, 768), BF),
            pltpu.VMEM((4, 2 * half, 128), F32),
        ],
        compiler_params=pltpu.CompilerParams(vmem_limit_bytes=40 << 20),
        name="attention_grads",
    )(keep, came)


def matmul(left, right, dims):
    return lax.dot_general(left, right, ((dims[:1], dims[1:]), ((), ())), preferred_element_type=F32)


def on_device(acts, perturb, dy, norm_gain, w_qkv, w_out):
    tensor, member, image = [lax.axis_index(axis) for axis in AXES]
    own_y, core = image // 2, image % 2
    first, stays = core == 0, core == tensor % 2
    features = acts.shape[3]
    heads, head_size = w_qkv.shape[2], w_qkv.shape[4]

    dy_own = swapped(dy[0, 0], stays)

    raw = w_qkv[0].transpose(0, 2, 1, 3).reshape(-1, head_size)
    w_back = w_out[0].reshape(heads * head_size, features)
    tiles = w_back.reshape(-1, 8, features // 128, 128).transpose(0, 2, 1, 3).reshape(-1, 128)
    eighth = core * 4 + own_y
    piece = jnp.concatenate(
        [
            lax.dynamic_slice_in_dim(array, eighth * (array.shape[0] // 8), array.shape[0] // 8, 0)
            for array in (raw, tiles)
        ],
        axis=0,
    )
    perturb, piece = together(perturb, piece)
    piece_other = send(piece, ZL)

    rows = lax.all_to_all(
        jnp.broadcast_to(perturb, (16, *perturb.shape)), AXES, 0, 0, axis_index_groups=BLOCKS
    )
    dy_left, dy_right, dy_far = [send(dy_own, X[step]) for step in (1, -1, 2)]
    rows, piece_other, dy_left, dy_right = together(rows, piece_other, dy_left, dy_right)
    inputs = inputs_of(rows, acts[0, 0], first)

    pieces = [piece_other] + [send(piece_other, Y[step]) for step in (1, -1, 2)]
    in_own = swapped(inputs, stays)
    in_own, dy_far, raw = together(in_own, dy_far, raw)
    w_mat = own_weights(raw)
    in_left, in_right = send(in_own, X[1]), send(in_own, X[-1])
    half = in_own.shape[0] // 2
    far_up, far_down = send(in_left[:half], X[1]), send(in_right[half:], X[-1])
    in_left, in_right, *pieces = together(in_left, in_right, *pieces)
    mat_half, back_half = other_weights(pieces, own_y)

    w_back_other, w_mat_other = joined(back_half, first), joined(mat_half, first)

    rows_dy = jnp.concatenate([dy_own, dy_left, dy_right, dy_far], axis=0)
    normed, rows_in, spread = normed_rows([in_own, in_left, in_right, far_up, far_down], norm_gain)
    up = matmul(rows_dy, w_back, (1, 1)).astype(BF)
    packed = matmul(normed, w_mat, (1, 0)).astype(BF)
    up_other = matmul(rows_dy, w_back_other, (1, 1)).astype(BF)
    packed_other = matmul(normed, w_mat_other, (1, 0)).astype(BF)
    both = jnp.concatenate([packed, up], axis=1)
    both_other = jnp.concatenate([packed_other, up_other], axis=1)
    keep = jnp.where(first, both, both_other)
    came = send(jnp.where(first, both_other, both), CORE)
    mine, theirs = attention_grads(keep, came)
    came = send(theirs, CORE)
    grads_own = jnp.where(first, mine, came)
    grads_other = jnp.where(first, came, mine)

    def result_of(grads, start, stop):
        return result_part(
            grads,
            [packed, packed_other],
            [w_mat, w_mat_other],
            rows_in,
            spread,
            norm_gain,
            dy_own,
            start,
            stop,
        )

    def over_x(value):
        count = value.shape[0] // 4
        total = value[:count].astype(F32)
        for place, step in ((3, 2), (1, -1), (2, 1)):
            piece = value[place * count : (place + 1) * count]
            total = total + send(piece, X[step]).astype(F32)
        return total.astype(BF)

    def over(value, ring, own, dim):
        total = lax.dynamic_index_in_dim(value, own, dim, keepdims=False).astype(F32)
        for step in (2, 1, -1):
            piece = lax.dynamic_index_in_dim(value, (own + step) % 4, dim, keepdims=False)
            total = total + send(piece, ring[step]).astype(F32)
        return total

    cut = 1280
    result_a = result_of([grads_own, grads_other], 0, cut)
    result_a, grads_own, grads_other = together(result_a, grads_own, grads_other)
    result_b = result_of([grads_own, grads_other], cut, features)
    part_a = together(over_x(result_a))[0]
    part_b = over(result_b.reshape(4, 4, 4, 8, -1), Y, own_y, 2).astype(BF)
    part_a = over(part_a.reshape(4, 4, 8, -1), Y, own_y, 1)
    part_b = over_x(part_b.reshape(128, -1)).reshape(4, 8, -1)
    total = jnp.concatenate([part_a.astype(BF), part_b], axis=-1)
    total = over(total, Z, member, 0)
    total = total.reshape(2, 4, features)
    near = jnp.where(tensor % 2 == 0, total[0], total[1])
    across = jnp.where(tensor % 2 == 0, total[1], total[0])
    return swapped(near, stays) + send(across, TURN)


def solution(mesh):
    in_specs = (
        P("member", "image", "tensor", None),
        P(("tensor", "member", "image"), None),
        P("member", "image", "tensor", None),
        P("member", None),
        P("member", None, "tensor", None, None),
        P("member", "tensor", None, None),
    )
    out_specs = P(("tensor", "member", "image"), None)
    return jax.shard_map(
        on_device, mesh=mesh, in_specs=in_specs, out_specs=out_specs, check_vma=False
    )
```

```python
import functools
import math

import jax
import jax.numpy as jnp
from jax import lax
from jax.experimental import pallas as pl
from jax.experimental.pallas import tpu as pltpu
from jax.sharding import PartitionSpec as P

AXES = ("tensor", "member", "image")
BF = jnp.bfloat16
F32 = jnp.float32


def routes(move):
    pairs = []
    for x in range(4):
        for zl in range(2):
            for zh in range(4):
                for y in range(4):
                    for c in range(2):
                        nx, nzl, nzh, ny, nc = move(x, zl, zh, y, c)
                        pairs.append(
                            (
                                ((x * 2 + zl) * 4 + zh) * 8 + y * 2 + c,
                                (((nx % 4) * 2 + nzl) * 4 + nzh % 4) * 8 + (ny % 4) * 2 + nc,
                            )
                        )
    return [(source, target) for source, target in pairs if source != target]


SWAP = routes(lambda x, zl, zh, y, c: (x, c, zh, y, zl))
OWNER = {
    d: routes(lambda x, zl, zh, y, c, d=d: (x, c, zh + d, y, zl)) for d in (-1, 1, 2)
}
OTHER_OWNER = {
    d: routes(lambda x, zl, zh, y, c, d=d: (x, c, zh + d, y, 1 - zl)) for d in (-1, 0, 1, 2)
}
CORE = routes(lambda x, zl, zh, y, c: (x, zl, zh, y, 1 - c))
ZL = routes(lambda x, zl, zh, y, c: (x, 1 - zl, zh, y, c))
X = {d: routes(lambda x, zl, zh, y, c, d=d: (x + d, zl, zh, y, c)) for d in (-1, 1, 2)}

Y = {d: routes(lambda x, zl, zh, y, c, d=d: (x, zl, zh, y + d, c)) for d in (-1, 1, 2)}


BLOCKS = [
    [(t * 4 + zh) * 8 + y * 2 + c for zh in range(4) for y in range(4)]
    for t in range(8)
    for c in range(2)
]


def send(value, pairs):
    return lax.ppermute(value, AXES, pairs)


def together(*values):
    return lax.optimization_barrier(values)


def swapped(value, stays):
    return jnp.where(stays, value, send(value, SWAP))


def rows_of_weights(raw, scratch, rows):
    scratch[...] = raw.astype(F32)
    return [scratch[pl.ds(column, rows, stride=6), :].astype(BF) for column in range(6)]


def own_weights_body(raw_ref, out_ref, scratch):
    rows = out_ref.shape[0]
    for column, value in enumerate(rows_of_weights(raw_ref[...], scratch, rows)):
        out_ref[:, column * 128 : (column + 1) * 128] = value


def own_weights(raw):
    count, step = raw.shape[0] // 6, 400
    return pl.pallas_call(
        own_weights_body,
        grid=(count // step,),
        in_specs=[pl.BlockSpec((step * 6, 128), lambda i: (i, 0))],
        out_specs=pl.BlockSpec((step, 768), lambda i: (i, 0)),
        out_shape=jax.ShapeDtypeStruct((count, 768), BF),
        scratch_shapes=[pltpu.VMEM((step * 6, 128), F32)],
        compiler_params=pltpu.CompilerParams(vmem_limit_bytes=16 << 20),
        cost_estimate=pl.CostEstimate(flops=0, bytes_accessed=40 << 20, transcendentals=0),
        name="own_weights",
    )(raw)


def other_weights_body(place_ref, p0, p1, p2, p3, mat_ref, back_ref, scratch, scratch_back):
    for ref, step in ((p0, 0), (p1, 3), (p2, 1), (p3, 2)):
        place = (place_ref[0] + step) % 4
        at = pl.multiple_of(place * 400, 16)
        for column, value in enumerate(rows_of_weights(ref[:2400, :], scratch, 400)):
            mat_ref[pl.ds(at, 400), column * 128 : (column + 1) * 128] = value
        scratch_back[...] = ref[2400:, :].astype(F32)
        for pair in range(2):
            row = pl.multiple_of(place * 32 + pair * 16, 16)
            for column in range(25):
                upper = scratch_back[(pair * 50 + column) * 8 : (pair * 50 + column) * 8 + 8, :]
                lower = scratch_back[(pair * 50 + 25 + column) * 8 : (pair * 50 + 25 + column) * 8 + 8, :]
                back_ref[pl.ds(row, 16), column * 128 : (column + 1) * 128] = jnp.concatenate(
                    [upper, lower], axis=0
                ).astype(BF)


def other_weights(pieces, place):
    whole = pl.BlockSpec(memory_space=pltpu.VMEM)
    return pl.pallas_call(
        other_weights_body,
        in_specs=[pl.BlockSpec(memory_space=pltpu.SMEM), whole, whole, whole, whole],
        out_specs=[whole, whole],
        out_shape=[jax.ShapeDtypeStruct((1600, 768), BF), jax.ShapeDtypeStruct((128, 3200), BF)],
        scratch_shapes=[pltpu.VMEM((2400, 128), F32), pltpu.VMEM((800, 128), F32)],
        compiler_params=pltpu.CompilerParams(vmem_limit_bytes=32 << 20),
        cost_estimate=pl.CostEstimate(flops=0, bytes_accessed=40 << 20, transcendentals=0),
        name="other_weights",
    )(place.reshape(1), *pieces)


def normed_body(own, left, right, far_up, far_down, gains_ref, normed_ref, rows_ref, spread_ref):
    start = 0
    for ref in (own, left, right, far_up, far_down):
        for part in range(ref.shape[0] // 64):
            values = ref[part * 64 : part * 64 + 64, :]
            floats = values.astype(F32)
            spread = jnp.sqrt(jnp.mean(floats * floats, axis=-1, keepdims=True) + 1e-06)
            at = slice(start, start + 64)
            normed_ref[at, :] = (floats / spread * gains_ref[...]).astype(BF)
            rows_ref[at, :] = values
            spread_ref[at, :] = jnp.broadcast_to(spread, (64, 128))
            start += 64


def normed_rows(pieces, gains):
    whole = pl.BlockSpec(memory_space=pltpu.VMEM)
    return pl.pallas_call(
        normed_body,
        in_specs=[whole] * 6,
        out_specs=[whole] * 3,
        out_shape=[
            jax.ShapeDtypeStruct((512, 3200), BF),
            jax.ShapeDtypeStruct((512, 3200), BF),
            jax.ShapeDtypeStruct((512, 128), F32),
        ],
        compiler_params=pltpu.CompilerParams(vmem_limit_bytes=40 << 20),
        cost_estimate=pl.CostEstimate(flops=0, bytes_accessed=40 << 20, transcendentals=0),
        name="normed_rows",
    )(*pieces, gains)


def result_body(g_own, g_other, p_own, p_other, w_own, w_other, rows, spread, gains, own_dy, out, along_ref):
    features = 3200

    @pl.when(pl.program_id(0) == 0)
    def _():
        along = 0.0
        for grads, values in ((g_own, p_own), (g_other, p_other)):
            along = along + jnp.sum(
                grads[...].astype(F32) * values[...].astype(F32), axis=-1, keepdims=True
            )
        inverse = 1.0 / spread[...]
        along_ref[0] = inverse
        along_ref[1] = along * inverse * inverse / features

    grad = matmul(g_own[...], w_own[...], (1, 1)).astype(BF).astype(F32)
    grad = grad + matmul(g_other[...], w_other[...], (1, 1)).astype(BF).astype(F32)
    inverse, along = along_ref[0, :, :1], along_ref[1, :, :1]
    value = gains[...] * grad * inverse - rows[...].astype(F32) * along
    count = own_dy.shape[0]
    out[:count, :] = (value[:count] + own_dy[...].astype(F32)).astype(BF)
    out[count:, :] = value[count:].astype(BF)


def result_rows(grads, values, weights, rows, spread, gains, own_dy):
    tile = 640
    count, features = rows.shape
    whole = pl.BlockSpec(memory_space=pltpu.VMEM)
    weight = pl.BlockSpec((tile, 768), lambda i: (i, 0))
    return pl.pallas_call(
        result_body,
        grid=(features // tile,),
        in_specs=[
            whole,
            whole,
            whole,
            whole,
            weight,
            weight,
            pl.BlockSpec((count, tile), lambda i: (0, i)),
            whole,
            pl.BlockSpec((1, tile), lambda i: (0, i)),
            pl.BlockSpec((own_dy.shape[0], tile), lambda i: (0, i)),
        ],
        out_specs=pl.BlockSpec((count, tile), lambda i: (0, i)),
        out_shape=jax.ShapeDtypeStruct((count, features), BF),
        scratch_shapes=[pltpu.VMEM((2, count, 128), F32)],
        compiler_params=pltpu.CompilerParams(vmem_limit_bytes=56 << 20),
        name="result_rows",
    )(*grads, *values, *weights, rows, spread, gains, own_dy)


def joined_body(first_ref, mine, came, out):
    half = mine.shape[0]

    @pl.when(first_ref[0] == 1)
    def _():
        out[:half, :] = mine[...]
        out[half:, :] = came[...]

    @pl.when(first_ref[0] == 0)
    def _():
        out[:half, :] = came[...]
        out[half:, :] = mine[...]


def joined(mine, first):
    whole = pl.BlockSpec(memory_space=pltpu.VMEM)
    return pl.pallas_call(
        joined_body,
        in_specs=[pl.BlockSpec(memory_space=pltpu.SMEM), whole, whole],
        out_specs=whole,
        out_shape=jax.ShapeDtypeStruct((2 * mine.shape[0], mine.shape[1]), BF),
        compiler_params=pltpu.CompilerParams(vmem_limit_bytes=32 << 20),
        name="joined",
    )(first.astype(jnp.int32).reshape(1), mine, send(mine, CORE))


def inputs_body(first_ref, rows, other, acts, out):
    step = rows.shape[1]
    for group in range(0, rows.shape[0], 2):
        parts = []
        for index in (group, group + 1):
            mine, came = rows[index].astype(F32), other[index].astype(F32)
            parts.append(jnp.where(first_ref[0] == 1, mine, came))
            parts.append(jnp.where(first_ref[0] == 1, came, mine))
        at = slice(2 * step * group, 2 * step * (group + 2))
        out[at, :] = (acts[at, :].astype(F32) + jnp.concatenate(parts, axis=0)).astype(BF)


def inputs_of(rows, acts, first):
    whole = pl.BlockSpec(memory_space=pltpu.VMEM)
    return pl.pallas_call(
        inputs_body,
        in_specs=[pl.BlockSpec(memory_space=pltpu.SMEM), whole, whole, whole],
        out_specs=whole,
        out_shape=jax.ShapeDtypeStruct(acts.shape, BF),
        compiler_params=pltpu.CompilerParams(vmem_limit_bytes=16 << 20),
        name="inputs_of",
    )(first.astype(jnp.int32).reshape(1), rows, send(rows, CORE), acts)


def attention_body(keep_ref, came_ref, mine_ref, theirs_ref, table, grads, sums):
    half = keep_ref.shape[0]
    rows = 2 * half
    step = 256
    scale = 1.0 / math.sqrt(128)
    table[:half, :] = keep_ref[...]
    table[half:, :] = came_ref[...]
    heads = range(2)
    slots = [[slice(a, a + 128) for a in ((slot * 2 + head) * 128 for slot in range(4))] for head in heads]
    keys_t = [table[:, slots[head][1]].astype(F32).T.astype(BF) for head in heads]
    sums[...] = jnp.zeros_like(sums)

    def block(index, carry):
        here = pl.ds(pl.multiple_of(index * step, step), step)
        query = [table[here, slots[head][0]] for head in heads]
        upstream = [table[here, slots[head][3]] for head in heads]
        scores = [matmul(table[:, slots[head][1]], query[head], (1, 1)) for head in heads]
        through = [matmul(table[:, slots[head][2]], upstream[head], (1, 1)) for head in heads]
        for head in heads:
            expo = jnp.exp((scores[head] - jnp.max(scores[head], axis=0, keepdims=True)) * scale)
            attention = expo * (1.0 / jnp.sum(expo, axis=0, keepdims=True))
            centre = jnp.sum(attention * through[head], axis=0, keepdims=True)
            score_grad = (attention * (through[head] - centre) * scale).astype(BF)
            sums[2 * head] += matmul(score_grad, query[head], (1, 0))
            sums[2 * head + 1] += matmul(attention.astype(BF), upstream[head], (1, 0))
            grads[here, slots[head][0]] = matmul(keys_t[head], score_grad, (1, 0)).T.astype(BF)
        return carry

    lax.fori_loop(0, rows // step, block, 0)
    for head in heads:
        grads[:, slots[head][1]] = sums[2 * head].astype(BF)
        grads[:, slots[head][2]] = sums[2 * head + 1].astype(BF)
    mine_ref[...] = grads[:half, :]
    theirs_ref[...] = grads[half:, :]


def attention_grads(keep, came):
    half = keep.shape[0]
    whole = pl.BlockSpec(memory_space=pltpu.VMEM)
    return pl.pallas_call(
        attention_body,
        in_specs=[whole, whole],
        out_specs=[whole, whole],
        out_shape=[jax.ShapeDtypeStruct((half, 768), BF)] * 2,
        scratch_shapes=[
            pltpu.VMEM((2 * half, 1024), BF),
            pltpu.VMEM((2 * half, 768), BF),
            pltpu.VMEM((4, 2 * half, 128), F32),
        ],
        compiler_params=pltpu.CompilerParams(vmem_limit_bytes=40 << 20),
        name="attention_grads",
    )(keep, came)


def matmul(left, right, dims):
    return lax.dot_general(left, right, ((dims[:1], dims[1:]), ((), ())), preferred_element_type=F32)


def on_device(acts, perturb, dy, norm_gain, w_qkv, w_out):
    tensor, member, image = [lax.axis_index(axis) for axis in AXES]
    own_y, core = image // 2, image % 2
    first, stays = core == 0, core == tensor % 2
    features = acts.shape[3]
    heads, head_size = w_qkv.shape[2], w_qkv.shape[4]

    dy_own = swapped(dy[0, 0], stays)

    raw = w_qkv[0].transpose(0, 2, 1, 3).reshape(-1, head_size)
    w_back = w_out[0].reshape(heads * head_size, features)
    tiles = w_back.reshape(-1, 8, features // 128, 128).transpose(0, 2, 1, 3).reshape(-1, 128)
    eighth = core * 4 + own_y
    piece = jnp.concatenate(
        [
            lax.dynamic_slice_in_dim(array, eighth * (array.shape[0] // 8), array.shape[0] // 8, 0)
            for array in (raw, tiles)
        ],
        axis=0,
    )
    perturb, piece = together(perturb, piece)
    piece, dy_own = together(piece, dy_own)
    piece_other = send(piece, ZL)

    rows = lax.all_to_all(
        jnp.broadcast_to(perturb, (16, *perturb.shape)), AXES, 0, 0, axis_index_groups=BLOCKS
    )
    dy_left, dy_right, dy_far = [send(dy_own, X[step]) for step in (1, -1, 2)]
    rows, piece_other, dy_left, dy_right = together(rows, piece_other, dy_left, dy_right)
    inputs = inputs_of(rows, acts[0, 0], first)

    pieces = [piece_other] + [send(piece_other, Y[step]) for step in (1, -1, 2)]
    in_own = swapped(inputs, stays)
    in_own, dy_far, raw = together(in_own, dy_far, raw)
    w_mat = own_weights(raw)
    in_left, in_right = send(in_own, X[1]), send(in_own, X[-1])
    half = in_own.shape[0] // 2
    far_up, far_down = send(in_left[:half], X[1]), send(in_right[half:], X[-1])
    in_left, in_right, *pieces = together(in_left, in_right, *pieces)
    mat_half, back_half = other_weights(pieces, own_y)

    w_back_other, w_mat_other = joined(back_half, first), joined(mat_half, first)

    rows_dy = jnp.concatenate([dy_own, dy_left, dy_right, dy_far], axis=0)
    normed, rows_in, spread = normed_rows([in_own, in_left, in_right, far_up, far_down], norm_gain)
    up = matmul(rows_dy, w_back, (1, 1)).astype(BF)
    packed = matmul(normed, w_mat, (1, 0)).astype(BF)
    up_other = matmul(rows_dy, w_back_other, (1, 1)).astype(BF)
    packed_other = matmul(normed, w_mat_other, (1, 0)).astype(BF)
    both = jnp.concatenate([packed, up], axis=1)
    both_other = jnp.concatenate([packed_other, up_other], axis=1)
    keep = jnp.where(first, both, both_other)
    came = send(jnp.where(first, both_other, both), CORE)
    mine, theirs = attention_grads(keep, came)
    came = send(theirs, CORE)
    grads_own = jnp.where(first, mine, came)
    grads_other = jnp.where(first, came, mine)

    result = result_rows(
        [grads_own, grads_other],
        [packed, packed_other],
        [w_mat, w_mat_other],
        rows_in,
        spread,
        norm_gain,
        dy_own,
    )

    def over_x(value):
        count = value.shape[0] // 4
        total = value[:count].astype(F32)
        for place, step in ((3, 2), (1, -1), (2, 1)):
            piece = value[place * count : (place + 1) * count]
            total = total + send(piece, X[step]).astype(F32)
        return total.astype(BF)

    def over(value, ring, own, dim):
        total = lax.dynamic_index_in_dim(value, own, dim, keepdims=False).astype(F32)
        for step in (2, 1, -1):
            piece = lax.dynamic_index_in_dim(value, (own + step) % 4, dim, keepdims=False)
            total = total + send(piece, ring[step]).astype(F32)
        return total

    cut = 1664
    part_a = together(over_x(result[:, :cut]))[0]
    part_b = over(result[:, cut:].reshape(4, 4, 4, 8, -1), Y, own_y, 2).astype(BF)
    part_a = over(part_a.reshape(4, 4, 8, -1), Y, own_y, 1)
    part_b = over_x(part_b.reshape(128, -1)).reshape(4, 8, -1)
    total = jnp.concatenate([part_a.astype(BF), part_b], axis=-1)
    total = total.reshape(4, 2, 4, features)
    by_core = tensor % 2
    sums = None
    for step in (0, 2, 1, -1):
        places = lax.dynamic_index_in_dim(total, (member + step) % 4, 0, keepdims=False)
        near = lax.dynamic_index_in_dim(places, by_core, 0, keepdims=False)
        across = lax.dynamic_index_in_dim(places, 1 - by_core, 0, keepdims=False)
        came = swapped(near, stays) if step == 0 else send(near, OWNER[step])
        came = came.astype(F32) + send(across, OTHER_OWNER[step]).astype(F32)
        sums = came if sums is None else sums + came
    return sums


def solution(mesh):
    in_specs = (
        P("member", "image", "tensor", None),
        P(("tensor", "member", "image"), None),
        P("member", "image", "tensor", None),
        P("member", None),
        P("member", None, "tensor", None, None),
        P("member", "tensor", None, None),
    )
    out_specs = P(("tensor", "member", "image"), None)
    return jax.shard_map(
        on_device, mesh=mesh, in_specs=in_specs, out_specs=out_specs, check_vma=False
    )
```

```python
import functools
import math

import jax
import jax.numpy as jnp
from jax import lax
from jax.experimental import pallas as pl
from jax.experimental.pallas import tpu as pltpu
from jax.sharding import PartitionSpec as P

AXES = ("tensor", "member", "image")
BF = jnp.bfloat16
F32 = jnp.float32


def routes(move):
    pairs = []
    for x in range(4):
        for zl in range(2):
            for zh in range(4):
                for y in range(4):
                    for c in range(2):
                        nx, nzl, nzh, ny, nc = move(x, zl, zh, y, c)
                        pairs.append(
                            (
                                ((x * 2 + zl) * 4 + zh) * 8 + y * 2 + c,
                                (((nx % 4) * 2 + nzl) * 4 + nzh % 4) * 8 + (ny % 4) * 2 + nc,
                            )
                        )
    return [(source, target) for source, target in pairs if source != target]


SWAP = routes(lambda x, zl, zh, y, c: (x, c, zh, y, zl))
OWNER = {
    d: routes(lambda x, zl, zh, y, c, d=d: (x, c, zh + d, y, zl)) for d in (-1, 1, 2)
}
OTHER_OWNER = {
    d: routes(lambda x, zl, zh, y, c, d=d: (x, c, zh + d, y, 1 - zl)) for d in (-1, 0, 1, 2)
}
CORE = routes(lambda x, zl, zh, y, c: (x, zl, zh, y, 1 - c))
ZL = routes(lambda x, zl, zh, y, c: (x, 1 - zl, zh, y, c))
X = {d: routes(lambda x, zl, zh, y, c, d=d: (x + d, zl, zh, y, c)) for d in (-1, 1, 2)}

Y = {d: routes(lambda x, zl, zh, y, c, d=d: (x, zl, zh, y + d, c)) for d in (-1, 1, 2)}


BLOCKS = [
    [(t * 4 + zh) * 8 + y * 2 + c for zh in range(4) for y in range(4)]
    for t in range(8)
    for c in range(2)
]


RINGS = [[0, 2, 4, 6], [1, 3, 5, 7]]


def send(value, pairs):
    return lax.ppermute(value, AXES, pairs)


def together(*values):
    return lax.optimization_barrier(values)


def swapped(value, stays):
    return jnp.where(stays, value, send(value, SWAP))


def rows_of_weights(raw, scratch, rows):
    scratch[...] = raw.astype(F32)
    return [scratch[pl.ds(column, rows, stride=6), :].astype(BF) for column in range(6)]


def own_weights_body(raw_ref, out_ref, scratch):
    rows = out_ref.shape[0]
    for column, value in enumerate(rows_of_weights(raw_ref[...], scratch, rows)):
        out_ref[:, column * 128 : (column + 1) * 128] = value


def own_weights(raw):
    count, step = raw.shape[0] // 6, 400
    return pl.pallas_call(
        own_weights_body,
        grid=(count // step,),
        in_specs=[pl.BlockSpec((step * 6, 128), lambda i: (i, 0))],
        out_specs=pl.BlockSpec((step, 768), lambda i: (i, 0)),
        out_shape=jax.ShapeDtypeStruct((count, 768), BF),
        scratch_shapes=[pltpu.VMEM((step * 6, 128), F32)],
        compiler_params=pltpu.CompilerParams(vmem_limit_bytes=16 << 20),
        cost_estimate=pl.CostEstimate(flops=0, bytes_accessed=40 << 20, transcendentals=0),
        name="own_weights",
    )(raw)


def other_weights_body(pieces, mat_ref, back_ref, scratch, scratch_back):
    for place in range(4):
        at = slice(place * 400, place * 400 + 400)
        for column, value in enumerate(rows_of_weights(pieces[place, :2400, :], scratch, 400)):
            mat_ref[at, column * 128 : (column + 1) * 128] = value
        scratch_back[...] = pieces[place, 2400:, :].astype(F32)
        for pair in range(2):
            row = place * 32 + pair * 16
            for column in range(25):
                upper = (pair * 50 + column) * 8
                lower = upper + 200
                back_ref[row : row + 16, column * 128 : (column + 1) * 128] = jnp.concatenate(
                    [scratch_back[upper : upper + 8, :], scratch_back[lower : lower + 8, :]], axis=0
                ).astype(BF)


def other_weights(pieces):
    whole = pl.BlockSpec(memory_space=pltpu.VMEM)
    return pl.pallas_call(
        other_weights_body,
        in_specs=[whole],
        out_specs=[whole, whole],
        out_shape=[jax.ShapeDtypeStruct((1600, 768), BF), jax.ShapeDtypeStruct((128, 3200), BF)],
        scratch_shapes=[pltpu.VMEM((2400, 128), F32), pltpu.VMEM((800, 128), F32)],
        compiler_params=pltpu.CompilerParams(vmem_limit_bytes=32 << 20),
        name="other_weights",
    )(pieces)


def normed_body(own, left, right, far_up, far_down, gains_ref, normed_ref, rows_ref, spread_ref):
    start = 0
    for ref in (own, left, right, far_up, far_down):
        for part in range(ref.shape[0] // 64):
            values = ref[part * 64 : part * 64 + 64, :]
            floats = values.astype(F32)
            spread = jnp.sqrt(jnp.mean(floats * floats, axis=-1, keepdims=True) + 1e-06)
            at = slice(start, start + 64)
            normed_ref[at, :] = (floats / spread * gains_ref[...]).astype(BF)
            rows_ref[at, :] = values
            spread_ref[at, :] = jnp.broadcast_to(spread, (64, 128))
            start += 64


def normed_rows(pieces, gains):
    whole = pl.BlockSpec(memory_space=pltpu.VMEM)
    return pl.pallas_call(
        normed_body,
        in_specs=[whole] * 6,
        out_specs=[whole] * 3,
        out_shape=[
            jax.ShapeDtypeStruct((512, 3200), BF),
            jax.ShapeDtypeStruct((512, 3200), BF),
            jax.ShapeDtypeStruct((512, 128), F32),
        ],
        compiler_params=pltpu.CompilerParams(vmem_limit_bytes=40 << 20),
        cost_estimate=pl.CostEstimate(flops=0, bytes_accessed=40 << 20, transcendentals=0),
        name="normed_rows",
    )(*pieces, gains)


def result_body(g_own, g_other, p_own, p_other, part_own, part_other, rows, spread, gains, own_dy, out):
    along = 0.0
    for grads, values in ((g_own, p_own), (g_other, p_other)):
        along = along + jnp.sum(
            grads[...].astype(F32) * values[...].astype(F32), axis=-1, keepdims=True
        )
    inverse = 1.0 / spread[:, :1]
    along = along * inverse * inverse / rows.shape[1]
    is_own = pl.program_id(0) == 0
    tile = 640
    for start in range(0, rows.shape[1], tile):
        at = slice(start, start + tile)
        grad = part_own[:, at].astype(F32) + part_other[:, at].astype(F32)
        value = gains[:, at] * grad * inverse - rows[:, at].astype(F32) * along
        value = value + jnp.where(is_own, own_dy[:, at].astype(F32), 0.0)
        out[:, at] = value.astype(BF)


def result_rows(grads, values, partials, rows, spread, gains, own_dy):
    count, features = rows.shape
    block = own_dy.shape[0]
    narrow = pl.BlockSpec((block, 768), lambda i: (i, 0))
    wide = pl.BlockSpec((block, features), lambda i: (i, 0))
    whole = pl.BlockSpec(memory_space=pltpu.VMEM)
    return pl.pallas_call(
        result_body,
        grid=(count // block,),
        in_specs=[narrow] * 4
        + [wide] * 3
        + [pl.BlockSpec((block, 128), lambda i: (i, 0)), whole, whole],
        out_specs=wide,
        out_shape=jax.ShapeDtypeStruct((count, features), BF),
        compiler_params=pltpu.CompilerParams(vmem_limit_bytes=24 << 20),
        name="result_rows",
    )(*grads, *values, *partials, rows, spread, gains, own_dy)


def joined_body(first_ref, mine, came, out):
    half = mine.shape[0]

    @pl.when(first_ref[0] == 1)
    def _():
        out[:half, :] = mine[...]
        out[half:, :] = came[...]

    @pl.when(first_ref[0] == 0)
    def _():
        out[:half, :] = came[...]
        out[half:, :] = mine[...]


def joined(mine, first):
    whole = pl.BlockSpec(memory_space=pltpu.VMEM)
    return pl.pallas_call(
        joined_body,
        in_specs=[pl.BlockSpec(memory_space=pltpu.SMEM), whole, whole],
        out_specs=whole,
        out_shape=jax.ShapeDtypeStruct((2 * mine.shape[0], mine.shape[1]), BF),
        compiler_params=pltpu.CompilerParams(vmem_limit_bytes=32 << 20),
        name="joined",
    )(first.astype(jnp.int32).reshape(1), mine, send(mine, CORE))


def inputs_body(first_ref, rows, other, acts, out):
    step = rows.shape[1]
    for group in range(0, rows.shape[0], 2):
        parts = []
        for index in (group, group + 1):
            mine, came = rows[index].astype(F32), other[index].astype(F32)
            parts.append(jnp.where(first_ref[0] == 1, mine, came))
            parts.append(jnp.where(first_ref[0] == 1, came, mine))
        at = slice(2 * step * group, 2 * step * (group + 2))
        out[at, :] = (acts[at, :].astype(F32) + jnp.concatenate(parts, axis=0)).astype(BF)


def inputs_of(rows, acts, first):
    whole = pl.BlockSpec(memory_space=pltpu.VMEM)
    return pl.pallas_call(
        inputs_body,
        in_specs=[pl.BlockSpec(memory_space=pltpu.SMEM), whole, whole, whole],
        out_specs=whole,
        out_shape=jax.ShapeDtypeStruct(acts.shape, BF),
        compiler_params=pltpu.CompilerParams(vmem_limit_bytes=16 << 20),
        name="inputs_of",
    )(first.astype(jnp.int32).reshape(1), rows, send(rows, CORE), acts)


def attention_body(keep_ref, came_ref, mine_ref, theirs_ref, table, grads, sums):
    half = keep_ref.shape[0]
    rows = 2 * half
    step = 256
    scale = 1.0 / math.sqrt(128)
    table[:half, :] = keep_ref[...]
    table[half:, :] = came_ref[...]
    heads = range(2)
    slots = [[slice(a, a + 128) for a in ((slot * 2 + head) * 128 for slot in range(4))] for head in heads]
    keys_t = [table[:, slots[head][1]].astype(F32).T.astype(BF) for head in heads]
    sums[...] = jnp.zeros_like(sums)

    def block(index, carry):
        here = pl.ds(pl.multiple_of(index * step, step), step)
        query = [table[here, slots[head][0]] for head in heads]
        upstream = [table[here, slots[head][3]] for head in heads]
        scores = [matmul(table[:, slots[head][1]], query[head], (1, 1)) for head in heads]
        through = [matmul(table[:, slots[head][2]], upstream[head], (1, 1)) for head in heads]
        for head in heads:
            expo = jnp.exp((scores[head] - jnp.max(scores[head], axis=0, keepdims=True)) * scale)
            attention = expo * (1.0 / jnp.sum(expo, axis=0, keepdims=True))
            centre = jnp.sum(attention * through[head], axis=0, keepdims=True)
            score_grad = (attention * (through[head] - centre) * scale).astype(BF)
            sums[2 * head] += matmul(score_grad, query[head], (1, 0))
            sums[2 * head + 1] += matmul(attention.astype(BF), upstream[head], (1, 0))
            grads[here, slots[head][0]] = matmul(keys_t[head], score_grad, (1, 0)).T.astype(BF)
        return carry

    lax.fori_loop(0, rows // step, block, 0)
    for head in heads:
        grads[:, slots[head][1]] = sums[2 * head].astype(BF)
        grads[:, slots[head][2]] = sums[2 * head + 1].astype(BF)
    mine_ref[...] = grads[:half, :]
    theirs_ref[...] = grads[half:, :]


def attention_grads(keep, came):
    half = keep.shape[0]
    whole = pl.BlockSpec(memory_space=pltpu.VMEM)
    return pl.pallas_call(
        attention_body,
        in_specs=[whole, whole],
        out_specs=[whole, whole],
        out_shape=[jax.ShapeDtypeStruct((half, 768), BF)] * 2,
        scratch_shapes=[
            pltpu.VMEM((2 * half, 1024), BF),
            pltpu.VMEM((2 * half, 768), BF),
            pltpu.VMEM((4, 2 * half, 128), F32),
        ],
        compiler_params=pltpu.CompilerParams(vmem_limit_bytes=40 << 20),
        name="attention_grads",
    )(keep, came)


def matmul(left, right, dims):
    return lax.dot_general(left, right, ((dims[:1], dims[1:]), ((), ())), preferred_element_type=F32)


def on_device(acts, perturb, dy, norm_gain, w_qkv, w_out):
    tensor, member, image = [lax.axis_index(axis) for axis in AXES]
    own_y, core = image // 2, image % 2
    first, stays = core == 0, core == tensor % 2
    features = acts.shape[3]
    heads, head_size = w_qkv.shape[2], w_qkv.shape[4]

    dy_own = swapped(dy[0, 0], stays)

    raw = w_qkv[0].transpose(0, 2, 1, 3).reshape(-1, head_size)
    w_back = w_out[0].reshape(heads * head_size, features)
    tiles = w_back.reshape(-1, 8, features // 128, 128).transpose(0, 2, 1, 3).reshape(-1, 128)
    eighth = core * 4 + own_y
    piece = jnp.concatenate(
        [
            lax.dynamic_slice_in_dim(array, eighth * (array.shape[0] // 8), array.shape[0] // 8, 0)
            for array in (raw, tiles)
        ],
        axis=0,
    )
    perturb, piece = together(perturb, piece)
    piece_other = send(piece, ZL)

    rows = lax.all_to_all(
        jnp.broadcast_to(perturb, (16, *perturb.shape)), AXES, 0, 0, axis_index_groups=BLOCKS
    )
    dy_left, dy_right = send(dy_own, X[1]), send(dy_own, X[-1])
    rows, piece_other, dy_left, dy_right = together(rows, piece_other, dy_left, dy_right)
    dy_far = send(dy_left, X[1])
    inputs = inputs_of(rows, acts[0, 0], first)

    pieces = lax.all_to_all(
        jnp.broadcast_to(piece_other, (4, *piece_other.shape)), "image", 0, 0, axis_index_groups=RINGS
    )
    in_own = swapped(inputs, stays)
    in_own, raw = together(in_own, raw)
    w_mat = own_weights(raw)
    in_left, in_right = send(in_own, X[1]), send(in_own, X[-1])
    half = in_own.shape[0] // 2
    far_up, far_down = send(in_left[:half], X[1]), send(in_right[half:], X[-1])
    in_left, in_right, pieces = together(in_left, in_right, pieces)
    mat_half, back_half = other_weights(pieces)

    w_back_other, w_mat_other = joined(back_half, first), joined(mat_half, first)

    rows_dy = jnp.concatenate([dy_own, dy_left, dy_right, dy_far], axis=0)
    normed, rows_in, spread = normed_rows([in_own, in_left, in_right, far_up, far_down], norm_gain)
    up = matmul(rows_dy, w_back, (1, 1)).astype(BF)
    packed = matmul(normed, w_mat, (1, 0)).astype(BF)
    up_other = matmul(rows_dy, w_back_other, (1, 1)).astype(BF)
    packed_other = matmul(normed, w_mat_other, (1, 0)).astype(BF)
    both = jnp.concatenate([packed, up], axis=1)
    both_other = jnp.concatenate([packed_other, up_other], axis=1)
    keep = jnp.where(first, both, both_other)
    came = send(jnp.where(first, both_other, both), CORE)
    mine, theirs = attention_grads(keep, came)
    came = send(theirs, CORE)
    grads_own = jnp.where(first, mine, came)
    grads_other = jnp.where(first, came, mine)

    partials = [
        lax.optimization_barrier(matmul(grads_own, w_mat, (1, 1)).astype(BF)),
        lax.optimization_barrier(matmul(grads_other, w_mat_other, (1, 1)).astype(BF)),
    ]
    result = result_rows(
        [grads_own, grads_other],
        [packed, packed_other],
        partials,
        rows_in,
        spread,
        norm_gain,
        dy_own,
    )

    def over_x(value):
        count = value.shape[0] // 4
        total = value[:count].astype(F32)
        for place, step in ((3, 2), (1, -1), (2, 1)):
            piece = value[place * count : (place + 1) * count]
            total = total + send(piece, X[step]).astype(F32)
        return total.astype(BF)

    def over(value, ring, own, dim):
        total = lax.dynamic_index_in_dim(value, own, dim, keepdims=False).astype(F32)
        for step in (2, 1, -1):
            piece = lax.dynamic_index_in_dim(value, (own + step) % 4, dim, keepdims=False)
            total = total + send(piece, ring[step]).astype(F32)
        return total

    cut = 1664
    part_a = together(over_x(result[:, :cut]))[0]
    part_b = over(result[:, cut:].reshape(4, 4, 4, 8, -1), Y, own_y, 2).astype(BF)
    part_a = over(part_a.reshape(4, 4, 8, -1), Y, own_y, 1)
    part_b = over_x(part_b.reshape(128, -1)).reshape(4, 8, -1)
    total = jnp.concatenate([part_a.astype(BF), part_b], axis=-1)
    total = total.reshape(4, 2, 4, features)
    by_core = tensor % 2
    sums = None
    for step in (0, 2, 1, -1):
        places = lax.dynamic_index_in_dim(total, (member + step) % 4, 0, keepdims=False)
        near = lax.dynamic_index_in_dim(places, by_core, 0, keepdims=False)
        across = lax.dynamic_index_in_dim(places, 1 - by_core, 0, keepdims=False)
        came = swapped(near, stays) if step == 0 else send(near, OWNER[step])
        came = came.astype(F32) + send(across, OTHER_OWNER[step]).astype(F32)
        sums = came if sums is None else sums + came
    return sums


def solution(mesh):
    in_specs = (
        P("member", "image", "tensor", None),
        P(("tensor", "member", "image"), None),
        P("member", "image", "tensor", None),
        P("member", None),
        P("member", None, "tensor", None, None),
        P("member", "tensor", None, None),
    )
    out_specs = P(("tensor", "member", "image"), None)
    return jax.shard_map(
        on_device, mesh=mesh, in_specs=in_specs, out_specs=out_specs, check_vma=False
    )
```

```python
import functools
import math

import jax
import jax.numpy as jnp
from jax import lax
from jax.experimental import pallas as pl
from jax.experimental.pallas import tpu as pltpu
from jax.sharding import PartitionSpec as P

AXES = ("tensor", "member", "image")
BF = jnp.bfloat16
F32 = jnp.float32


def routes(move):
    pairs = []
    for x in range(4):
        for zl in range(2):
            for zh in range(4):
                for y in range(4):
                    for c in range(2):
                        nx, nzl, nzh, ny, nc = move(x, zl, zh, y, c)
                        pairs.append(
                            (
                                ((x * 2 + zl) * 4 + zh) * 8 + y * 2 + c,
                                (((nx % 4) * 2 + nzl) * 4 + nzh % 4) * 8 + (ny % 4) * 2 + nc,
                            )
                        )
    return [(source, target) for source, target in pairs if source != target]


SWAP = routes(lambda x, zl, zh, y, c: (x, c, zh, y, zl))
OWNER = {
    d: routes(lambda x, zl, zh, y, c, d=d: (x, c, zh + d, y, zl)) for d in (-1, 1, 2)
}
OTHER_OWNER = {
    d: routes(lambda x, zl, zh, y, c, d=d: (x, c, zh + d, y, 1 - zl)) for d in (-1, 0, 1, 2)
}
CORE = routes(lambda x, zl, zh, y, c: (x, zl, zh, y, 1 - c))
ZL = routes(lambda x, zl, zh, y, c: (x, 1 - zl, zh, y, c))
X = {d: routes(lambda x, zl, zh, y, c, d=d: (x + d, zl, zh, y, c)) for d in (-1, 1, 2)}

Y = {d: routes(lambda x, zl, zh, y, c, d=d: (x, zl, zh, y + d, c)) for d in (-1, 1, 2)}


BLOCKS = [
    [(t * 4 + zh) * 8 + y * 2 + c for zh in range(4) for y in range(4)]
    for t in range(8)
    for c in range(2)
]


def send(value, pairs):
    return lax.ppermute(value, AXES, pairs)


def together(*values):
    return lax.optimization_barrier(values)


def swapped(value, stays):
    return jnp.where(stays, value, send(value, SWAP))


def rows_of_weights(raw, scratch, rows):
    scratch[...] = raw.astype(F32)
    return [scratch[pl.ds(column, rows, stride=6), :].astype(BF) for column in range(6)]


def own_weights_body(raw_ref, out_ref, scratch):
    rows = out_ref.shape[0]
    for column, value in enumerate(rows_of_weights(raw_ref[...], scratch, rows)):
        out_ref[:, column * 128 : (column + 1) * 128] = value


def own_weights(raw):
    count, step = raw.shape[0] // 6, 400
    return pl.pallas_call(
        own_weights_body,
        grid=(count // step,),
        in_specs=[pl.BlockSpec((step * 6, 128), lambda i: (i, 0))],
        out_specs=pl.BlockSpec((step, 768), lambda i: (i, 0)),
        out_shape=jax.ShapeDtypeStruct((count, 768), BF),
        scratch_shapes=[pltpu.VMEM((step * 6, 128), F32)],
        compiler_params=pltpu.CompilerParams(vmem_limit_bytes=16 << 20),
        cost_estimate=pl.CostEstimate(flops=0, bytes_accessed=40 << 20, transcendentals=0),
        name="own_weights",
    )(raw)


def other_weights_body(place_ref, p0, p1, p2, p3, mat_ref, back_ref, scratch, scratch_back):
    for ref, step in ((p0, 0), (p1, 3), (p2, 1), (p3, 2)):
        place = (place_ref[0] + step) % 4
        at = pl.multiple_of(place * 400, 16)
        for column, value in enumerate(rows_of_weights(ref[:2400, :], scratch, 400)):
            mat_ref[pl.ds(at, 400), column * 128 : (column + 1) * 128] = value
        scratch_back[...] = ref[2400:, :].astype(F32)
        for pair in range(2):
            row = pl.multiple_of(place * 32 + pair * 16, 16)
            for column in range(25):
                upper = scratch_back[(pair * 50 + column) * 8 : (pair * 50 + column) * 8 + 8, :]
                lower = scratch_back[(pair * 50 + 25 + column) * 8 : (pair * 50 + 25 + column) * 8 + 8, :]
                back_ref[pl.ds(row, 16), column * 128 : (column + 1) * 128] = jnp.concatenate(
                    [upper, lower], axis=0
                ).astype(BF)


def other_weights(pieces, place):
    whole = pl.BlockSpec(memory_space=pltpu.VMEM)
    return pl.pallas_call(
        other_weights_body,
        in_specs=[pl.BlockSpec(memory_space=pltpu.SMEM), whole, whole, whole, whole],
        out_specs=[whole, whole],
        out_shape=[jax.ShapeDtypeStruct((1600, 768), BF), jax.ShapeDtypeStruct((128, 3200), BF)],
        scratch_shapes=[pltpu.VMEM((2400, 128), F32), pltpu.VMEM((800, 128), F32)],
        compiler_params=pltpu.CompilerParams(vmem_limit_bytes=32 << 20),
        cost_estimate=pl.CostEstimate(flops=0, bytes_accessed=40 << 20, transcendentals=0),
        name="other_weights",
    )(place.reshape(1), *pieces)


def normed_body(own, left, right, far, gains_ref, normed_ref, rows_ref, spread_ref):
    start = 0
    for ref in (own, left, right, far):
        for part in range(ref.shape[0] // 64):
            values = ref[part * 64 : part * 64 + 64, :]
            floats = values.astype(F32)
            spread = jnp.sqrt(jnp.mean(floats * floats, axis=-1, keepdims=True) + 1e-06)
            at = slice(start, start + 64)
            normed_ref[at, :] = (floats / spread * gains_ref[...]).astype(BF)
            rows_ref[at, :] = values
            spread_ref[at, :] = jnp.broadcast_to(spread, (64, 128))
            start += 64


def normed_rows(pieces, gains):
    whole = pl.BlockSpec(memory_space=pltpu.VMEM)
    return pl.pallas_call(
        normed_body,
        in_specs=[whole] * 5,
        out_specs=[whole] * 3,
        out_shape=[
            jax.ShapeDtypeStruct((512, 3200), BF),
            jax.ShapeDtypeStruct((512, 3200), BF),
            jax.ShapeDtypeStruct((512, 128), F32),
        ],
        compiler_params=pltpu.CompilerParams(vmem_limit_bytes=40 << 20),
        cost_estimate=pl.CostEstimate(flops=0, bytes_accessed=40 << 20, transcendentals=0),
        name="normed_rows",
    )(*pieces, gains)


def result_body(g_own, g_other, p_own, p_other, part_own, part_other, rows, spread, gains, own_dy, out):
    along = 0.0
    for grads, values in ((g_own, p_own), (g_other, p_other)):
        along = along + jnp.sum(
            grads[...].astype(F32) * values[...].astype(F32), axis=-1, keepdims=True
        )
    inverse = 1.0 / spread[:, :1]
    along = along * inverse * inverse / rows.shape[1]
    is_own = pl.program_id(0) == 0
    tile = 640
    for start in range(0, rows.shape[1], tile):
        at = slice(start, start + tile)
        grad = part_own[:, at].astype(F32) + part_other[:, at].astype(F32)
        value = gains[:, at] * grad * inverse - rows[:, at].astype(F32) * along
        value = value + jnp.where(is_own, own_dy[:, at].astype(F32), 0.0)
        out[:, at] = value.astype(BF)


def result_rows(grads, values, partials, rows, spread, gains, own_dy):
    count, features = rows.shape
    block = own_dy.shape[0]
    narrow = pl.BlockSpec((block, 768), lambda i: (i, 0))
    wide = pl.BlockSpec((block, features), lambda i: (i, 0))
    whole = pl.BlockSpec(memory_space=pltpu.VMEM)
    return pl.pallas_call(
        result_body,
        grid=(count // block,),
        in_specs=[narrow] * 4
        + [wide] * 3
        + [pl.BlockSpec((block, 128), lambda i: (i, 0)), whole, whole],
        out_specs=wide,
        out_shape=jax.ShapeDtypeStruct((count, features), BF),
        compiler_params=pltpu.CompilerParams(vmem_limit_bytes=24 << 20),
        name="result_rows",
    )(*grads, *values, *partials, rows, spread, gains, own_dy)


def joined_body(first_ref, mine, came, out):
    half = mine.shape[0]

    @pl.when(first_ref[0] == 1)
    def _():
        out[:half, :] = mine[...]
        out[half:, :] = came[...]

    @pl.when(first_ref[0] == 0)
    def _():
        out[:half, :] = came[...]
        out[half:, :] = mine[...]


def joined(mine, came, first):
    whole = pl.BlockSpec(memory_space=pltpu.VMEM)
    return pl.pallas_call(
        joined_body,
        in_specs=[pl.BlockSpec(memory_space=pltpu.SMEM), whole, whole],
        out_specs=whole,
        out_shape=jax.ShapeDtypeStruct((2 * mine.shape[0], mine.shape[1]), BF),
        compiler_params=pltpu.CompilerParams(vmem_limit_bytes=32 << 20),
        name="joined",
    )(first.astype(jnp.int32).reshape(1), mine, came)


def attention_body(keep_ref, came_ref, mine_ref, theirs_ref, table, grads, sums):
    half = keep_ref.shape[0]
    rows = 2 * half
    step = 256
    scale = 1.0 / math.sqrt(128)
    table[:half, :] = keep_ref[...]
    table[half:, :] = came_ref[...]
    heads = range(2)
    slots = [[slice(a, a + 128) for a in ((slot * 2 + head) * 128 for slot in range(4))] for head in heads]
    keys_t = [table[:, slots[head][1]].astype(F32).T.astype(BF) for head in heads]
    sums[...] = jnp.zeros_like(sums)

    def block(index, carry):
        here = pl.ds(pl.multiple_of(index * step, step), step)
        query = [table[here, slots[head][0]] for head in heads]
        upstream = [table[here, slots[head][3]] for head in heads]
        scores = [matmul(table[:, slots[head][1]], query[head], (1, 1)) for head in heads]
        through = [matmul(table[:, slots[head][2]], upstream[head], (1, 1)) for head in heads]
        for head in heads:
            expo = jnp.exp((scores[head] - jnp.max(scores[head], axis=0, keepdims=True)) * scale)
            attention = expo * (1.0 / jnp.sum(expo, axis=0, keepdims=True))
            centre = jnp.sum(attention * through[head], axis=0, keepdims=True)
            score_grad = (attention * (through[head] - centre) * scale).astype(BF)
            sums[2 * head] += matmul(score_grad, query[head], (1, 0))
            sums[2 * head + 1] += matmul(attention.astype(BF), upstream[head], (1, 0))
            grads[here, slots[head][0]] = matmul(keys_t[head], score_grad, (1, 0)).T.astype(BF)
        return carry

    lax.fori_loop(0, rows // step, block, 0)
    for head in heads:
        grads[:, slots[head][1]] = sums[2 * head].astype(BF)
        grads[:, slots[head][2]] = sums[2 * head + 1].astype(BF)
    mine_ref[...] = grads[:half, :]
    theirs_ref[...] = grads[half:, :]


def attention_grads(keep, came):
    half = keep.shape[0]
    whole = pl.BlockSpec(memory_space=pltpu.VMEM)
    return pl.pallas_call(
        attention_body,
        in_specs=[whole, whole],
        out_specs=[whole, whole],
        out_shape=[jax.ShapeDtypeStruct((half, 768), BF)] * 2,
        scratch_shapes=[
            pltpu.VMEM((2 * half, 1024), BF),
            pltpu.VMEM((2 * half, 768), BF),
            pltpu.VMEM((4, 2 * half, 128), F32),
        ],
        compiler_params=pltpu.CompilerParams(vmem_limit_bytes=40 << 20),
        name="attention_grads",
    )(keep, came)


def matmul(left, right, dims):
    return lax.dot_general(left, right, ((dims[:1], dims[1:]), ((), ())), preferred_element_type=F32)


def on_device(acts, perturb, dy, norm_gain, w_qkv, w_out):
    tensor, member, image = [lax.axis_index(axis) for axis in AXES]
    own_y, core = image // 2, image % 2
    first, stays = core == 0, core == tensor % 2
    features = acts.shape[3]
    heads, head_size = w_qkv.shape[2], w_qkv.shape[4]

    dy_own = swapped(dy[0, 0], stays)

    rows = lax.all_to_all(
        jnp.broadcast_to(perturb, (16, *perturb.shape)), AXES, 0, 0, axis_index_groups=BLOCKS
    )
    rows, dy_own = together(rows, dy_own)
    other = send(rows, CORE)
    shared = jnp.stack([jnp.where(first, rows, other), jnp.where(first, other, rows)], axis=1)
    inputs = acts[0, 0].astype(F32) + shared.reshape(-1, features).astype(F32)
    inputs = inputs.astype(BF)

    raw = w_qkv[0].transpose(0, 2, 1, 3).reshape(-1, head_size)
    w_back = w_out[0].reshape(heads * head_size, features)
    tiles = w_back.reshape(-1, 8, features // 128, 128).transpose(0, 2, 1, 3).reshape(-1, 128)
    eighth = core * 4 + own_y
    piece = jnp.concatenate(
        [
            lax.dynamic_slice_in_dim(array, eighth * (array.shape[0] // 8), array.shape[0] // 8, 0)
            for array in (raw, tiles)
        ],
        axis=0,
    )
    piece, dy_own = together(piece, dy_own)
    piece_other = send(piece, ZL)

    dy_left, dy_right, dy_far = [send(dy_own, X[step]) for step in (1, -1, 2)]
    pieces = [piece_other] + [send(piece_other, Y[step]) for step in (1, -1, 2)]
    in_own = swapped(inputs, stays)
    in_own, raw = together(in_own, raw)
    w_mat = own_weights(raw)
    in_left, in_right, in_far = [send(in_own, X[step]) for step in (1, -1, 2)]
    mat_half, back_half = other_weights(pieces, own_y)

    def halves(mine):
        came = send(mine, CORE)
        return came, [jnp.where(first, mine, came), jnp.where(first, came, mine)]

    w_back_other = jnp.concatenate(halves(back_half)[1], axis=0)
    mat_came, low_high = halves(mat_half)

    rows_dy = jnp.concatenate([dy_own, dy_left, dy_right, dy_far], axis=0)
    normed, rows_in, spread = normed_rows([in_own, in_left, in_right, in_far], norm_gain)
    up = matmul(rows_dy, w_back, (1, 1)).astype(BF)
    packed = matmul(normed, w_mat, (1, 0)).astype(BF)
    up_other = matmul(rows_dy, w_back_other, (1, 1)).astype(BF)
    packed_other = matmul(normed, jnp.concatenate(low_high, axis=0), (1, 0)).astype(BF)
    both = jnp.concatenate([packed, up], axis=1)
    both_other = jnp.concatenate([packed_other, up_other], axis=1)
    keep = jnp.where(first, both, both_other)
    came = send(jnp.where(first, both_other, both), CORE)
    mine, theirs = attention_grads(keep, came)
    came = send(theirs, CORE)
    grads_own = jnp.where(first, mine, came)
    grads_other = jnp.where(first, came, mine)

    w_mat_other = joined(mat_half, mat_came, first)
    partials = [
        lax.optimization_barrier(matmul(grads_own, w_mat, (1, 1)).astype(BF)),
        lax.optimization_barrier(matmul(grads_other, w_mat_other, (1, 1)).astype(BF)),
    ]
    result = result_rows(
        [grads_own, grads_other],
        [packed, packed_other],
        partials,
        rows_in,
        spread,
        norm_gain,
        dy_own,
    )

    def over_x(value):
        count = value.shape[0] // 4
        total = value[:count].astype(F32)
        for place, step in ((3, 2), (1, -1), (2, 1)):
            piece = value[place * count : (place + 1) * count]
            total = total + send(piece, X[step]).astype(F32)
        return total.astype(BF)

    def over(value, ring, own, dim):
        total = lax.dynamic_index_in_dim(value, own, dim, keepdims=False).astype(F32)
        for step in (2, 1, -1):
            piece = lax.dynamic_index_in_dim(value, (own + step) % 4, dim, keepdims=False)
            total = total + send(piece, ring[step]).astype(F32)
        return total

    cut = 1664
    part_a = together(over_x(result[:, :cut]))[0]
    part_b = over(result[:, cut:].reshape(4, 4, 4, 8, -1), Y, own_y, 2).astype(BF)
    part_a = over(part_a.reshape(4, 4, 8, -1), Y, own_y, 1)
    part_b = over_x(part_b.reshape(128, -1)).reshape(4, 8, -1)
    total = jnp.concatenate([part_a.astype(BF), part_b], axis=-1)
    total = total.reshape(4, 2, 4, features)
    by_core = tensor % 2
    sums = None
    for step in (0, 2, 1, -1):
        places = lax.dynamic_index_in_dim(total, (member + step) % 4, 0, keepdims=False)
        near = lax.dynamic_index_in_dim(places, by_core, 0, keepdims=False)
        across = lax.dynamic_index_in_dim(places, 1 - by_core, 0, keepdims=False)
        came = swapped(near, stays) if step == 0 else send(near, OWNER[step])
        came = came.astype(F32) + send(across, OTHER_OWNER[step]).astype(F32)
        sums = came if sums is None else sums + came
    return sums


def solution(mesh):
    in_specs = (
        P("member", "image", "tensor", None),
        P(("tensor", "member", "image"), None),
        P("member", "image", "tensor", None),
        P("member", None),
        P("member", None, "tensor", None, None),
        P("member", "tensor", None, None),
    )
    out_specs = P(("tensor", "member", "image"), None)
    return jax.shard_map(
        on_device, mesh=mesh, in_specs=in_specs, out_specs=out_specs, check_vma=False
    )
```

```python
import functools
import math

import jax
import jax.numpy as jnp
from jax import lax
from jax.experimental import pallas as pl
from jax.experimental.pallas import tpu as pltpu
from jax.sharding import PartitionSpec as P

AXES = ("tensor", "member", "image")
BF = jnp.bfloat16
F32 = jnp.float32


def routes(move):
    pairs = []
    for x in range(4):
        for zl in range(2):
            for zh in range(4):
                for y in range(4):
                    for c in range(2):
                        nx, nzl, nzh, ny, nc = move(x, zl, zh, y, c)
                        pairs.append(
                            (
                                ((x * 2 + zl) * 4 + zh) * 8 + y * 2 + c,
                                (((nx % 4) * 2 + nzl) * 4 + nzh % 4) * 8 + (ny % 4) * 2 + nc,
                            )
                        )
    return [(source, target) for source, target in pairs if source != target]


SWAP = routes(lambda x, zl, zh, y, c: (x, c, zh, y, zl))
CORE = routes(lambda x, zl, zh, y, c: (x, zl, zh, y, 1 - c))
ZL = routes(lambda x, zl, zh, y, c: (x, 1 - zl, zh, y, c))
X = {d: routes(lambda x, zl, zh, y, c, d=d: (x + d, zl, zh, y, c)) for d in (-1, 1, 2)}

Z = {d: routes(lambda x, zl, zh, y, c, d=d: (x, zl, zh + d, y, c)) for d in (-1, 1, 2)}
Y = {d: routes(lambda x, zl, zh, y, c, d=d: (x, zl, zh, y + d, c)) for d in (-1, 1, 2)}


BLOCKS = [
    [(t * 4 + zh) * 8 + y * 2 + c for zh in range(4) for y in range(4)]
    for t in range(8)
    for c in range(2)
]


def send(value, pairs):
    return lax.ppermute(value, AXES, pairs)


def together(*values):
    return lax.optimization_barrier(values)


def swapped(value, stays):
    return jnp.where(stays, value, send(value, SWAP))


def rows_of_weights(raw, scratch, rows):
    scratch[...] = raw.astype(F32)
    return [scratch[pl.ds(column, rows, stride=6), :].astype(BF) for column in range(6)]


def own_weights_body(raw_ref, out_ref, scratch):
    rows = out_ref.shape[0]
    for column, value in enumerate(rows_of_weights(raw_ref[...], scratch, rows)):
        out_ref[:, column * 128 : (column + 1) * 128] = value


def own_weights(raw):
    count, step = raw.shape[0] // 6, 400
    return pl.pallas_call(
        own_weights_body,
        grid=(count // step,),
        in_specs=[pl.BlockSpec((step * 6, 128), lambda i: (i, 0))],
        out_specs=pl.BlockSpec((step, 768), lambda i: (i, 0)),
        out_shape=jax.ShapeDtypeStruct((count, 768), BF),
        scratch_shapes=[pltpu.VMEM((step * 6, 128), F32)],
        compiler_params=pltpu.CompilerParams(vmem_limit_bytes=16 << 20),
        cost_estimate=pl.CostEstimate(flops=0, bytes_accessed=40 << 20, transcendentals=0),
        name="own_weights",
    )(raw)


def other_weights_body(place_ref, p0, p1, p2, p3, mat_ref, back_ref, scratch, scratch_back):
    for ref, step in ((p0, 0), (p1, 3), (p2, 1), (p3, 2)):
        place = (place_ref[0] + step) % 4
        at = pl.multiple_of(place * 400, 16)
        for column, value in enumerate(rows_of_weights(ref[:2400, :], scratch, 400)):
            mat_ref[pl.ds(at, 400), column * 128 : (column + 1) * 128] = value
        scratch_back[...] = ref[2400:, :].astype(F32)
        for pair in range(2):
            row = pl.multiple_of(place * 32 + pair * 16, 16)
            for column in range(25):
                upper = scratch_back[(pair * 50 + column) * 8 : (pair * 50 + column) * 8 + 8, :]
                lower = scratch_back[(pair * 50 + 25 + column) * 8 : (pair * 50 + 25 + column) * 8 + 8, :]
                back_ref[pl.ds(row, 16), column * 128 : (column + 1) * 128] = jnp.concatenate(
                    [upper, lower], axis=0
                ).astype(BF)


def other_weights(pieces, place):
    whole = pl.BlockSpec(memory_space=pltpu.VMEM)
    return pl.pallas_call(
        other_weights_body,
        in_specs=[pl.BlockSpec(memory_space=pltpu.SMEM), whole, whole, whole, whole],
        out_specs=[whole, whole],
        out_shape=[jax.ShapeDtypeStruct((1600, 768), BF), jax.ShapeDtypeStruct((128, 3200), BF)],
        scratch_shapes=[pltpu.VMEM((2400, 128), F32), pltpu.VMEM((800, 128), F32)],
        compiler_params=pltpu.CompilerParams(vmem_limit_bytes=32 << 20),
        cost_estimate=pl.CostEstimate(flops=0, bytes_accessed=40 << 20, transcendentals=0),
        name="other_weights",
    )(place.reshape(1), *pieces)


def normed_body(own, left, right, far, gains_ref, normed_ref, rows_ref, spread_ref):
    start = 0
    for ref in (own, left, right, far):
        for part in range(ref.shape[0] // 64):
            values = ref[part * 64 : part * 64 + 64, :]
            floats = values.astype(F32)
            spread = jnp.sqrt(jnp.mean(floats * floats, axis=-1, keepdims=True) + 1e-06)
            at = slice(start, start + 64)
            normed_ref[at, :] = (floats / spread * gains_ref[...]).astype(BF)
            rows_ref[at, :] = values
            spread_ref[at, :] = jnp.broadcast_to(spread, (64, 128))
            start += 64


def normed_rows(pieces, gains):
    whole = pl.BlockSpec(memory_space=pltpu.VMEM)
    return pl.pallas_call(
        normed_body,
        in_specs=[whole] * 5,
        out_specs=[whole] * 3,
        out_shape=[
            jax.ShapeDtypeStruct((512, 3200), BF),
            jax.ShapeDtypeStruct((512, 3200), BF),
            jax.ShapeDtypeStruct((512, 128), F32),
        ],
        compiler_params=pltpu.CompilerParams(vmem_limit_bytes=16 << 20),
        cost_estimate=pl.CostEstimate(flops=0, bytes_accessed=16 << 20, transcendentals=0),
        name="normed_rows",
    )(*pieces, gains)


def result_body(g_own, g_other, p_own, p_other, part_own, part_other, rows, spread, gains, own_dy, out):
    along = 0.0
    for grads, values in ((g_own, p_own), (g_other, p_other)):
        along = along + jnp.sum(
            grads[...].astype(F32) * values[...].astype(F32), axis=-1, keepdims=True
        )
    inverse = 1.0 / spread[:, :1]
    along = along * inverse * inverse / rows.shape[1]
    is_own = pl.program_id(0) == 0
    tile = 640
    for start in range(0, rows.shape[1], tile):
        at = slice(start, start + tile)
        grad = part_own[:, at].astype(F32) + part_other[:, at].astype(F32)
        value = gains[:, at] * grad * inverse - rows[:, at].astype(F32) * along
        value = value + jnp.where(is_own, own_dy[:, at].astype(F32), 0.0)
        out[:, at] = value.astype(BF)


def result_rows(grads, values, partials, rows, spread, gains, own_dy):
    count, features = rows.shape
    block = own_dy.shape[0]
    narrow = pl.BlockSpec((block, 768), lambda i: (i, 0))
    wide = pl.BlockSpec((block, features), lambda i: (i, 0))
    whole = pl.BlockSpec(memory_space=pltpu.VMEM)
    return pl.pallas_call(
        result_body,
        grid=(count // block,),
        in_specs=[narrow] * 4
        + [wide] * 3
        + [pl.BlockSpec((block, 128), lambda i: (i, 0)), whole, whole],
        out_specs=wide,
        out_shape=jax.ShapeDtypeStruct((count, features), BF),
        compiler_params=pltpu.CompilerParams(vmem_limit_bytes=24 << 20),
        name="result_rows",
    )(*grads, *values, *partials, rows, spread, gains, own_dy)


def joined_body(first_ref, mine, came, out):
    half = mine.shape[0]

    @pl.when(first_ref[0] == 1)
    def _():
        out[:half, :] = mine[...]
        out[half:, :] = came[...]

    @pl.when(first_ref[0] == 0)
    def _():
        out[:half, :] = came[...]
        out[half:, :] = mine[...]


def joined(mine, came, first):
    whole = pl.BlockSpec(memory_space=pltpu.VMEM)
    return pl.pallas_call(
        joined_body,
        in_specs=[pl.BlockSpec(memory_space=pltpu.SMEM), whole, whole],
        out_specs=whole,
        out_shape=jax.ShapeDtypeStruct((2 * mine.shape[0], mine.shape[1]), BF),
        compiler_params=pltpu.CompilerParams(vmem_limit_bytes=32 << 20),
        name="joined",
    )(first.astype(jnp.int32).reshape(1), mine, came)


def attention_body(keep_ref, came_ref, mine_ref, theirs_ref, table, grads, sums):
    half = keep_ref.shape[0]
    rows = 2 * half
    step = 256
    scale = 1.0 / math.sqrt(128)
    table[:half, :] = keep_ref[...]
    table[half:, :] = came_ref[...]
    heads = range(2)
    slots = [[slice(a, a + 128) for a in ((slot * 2 + head) * 128 for slot in range(4))] for head in heads]
    keys_t = [table[:, slots[head][1]].astype(F32).T.astype(BF) for head in heads]
    sums[...] = jnp.zeros_like(sums)

    def block(index, carry):
        here = pl.ds(pl.multiple_of(index * step, step), step)
        query = [table[here, slots[head][0]] for head in heads]
        upstream = [table[here, slots[head][3]] for head in heads]
        scores = [matmul(table[:, slots[head][1]], query[head], (1, 1)) for head in heads]
        through = [matmul(table[:, slots[head][2]], upstream[head], (1, 1)) for head in heads]
        for head in heads:
            expo = jnp.exp((scores[head] - jnp.max(scores[head], axis=0, keepdims=True)) * scale)
            attention = expo * (1.0 / jnp.sum(expo, axis=0, keepdims=True))
            centre = jnp.sum(attention * through[head], axis=0, keepdims=True)
            score_grad = (attention * (through[head] - centre) * scale).astype(BF)
            sums[2 * head] += matmul(score_grad, query[head], (1, 0))
            sums[2 * head + 1] += matmul(attention.astype(BF), upstream[head], (1, 0))
            grads[here, slots[head][0]] = matmul(keys_t[head], score_grad, (1, 0)).T.astype(BF)
        return carry

    lax.fori_loop(0, rows // step, block, 0)
    for head in heads:
        grads[:, slots[head][1]] = sums[2 * head].astype(BF)
        grads[:, slots[head][2]] = sums[2 * head + 1].astype(BF)
    mine_ref[...] = grads[:half, :]
    theirs_ref[...] = grads[half:, :]


def attention_grads(keep, came):
    half = keep.shape[0]
    whole = pl.BlockSpec(memory_space=pltpu.VMEM)
    return pl.pallas_call(
        attention_body,
        in_specs=[whole, whole],
        out_specs=[whole, whole],
        out_shape=[jax.ShapeDtypeStruct((half, 768), BF)] * 2,
        scratch_shapes=[
            pltpu.VMEM((2 * half, 1024), BF),
            pltpu.VMEM((2 * half, 768), BF),
            pltpu.VMEM((4, 2 * half, 128), F32),
        ],
        compiler_params=pltpu.CompilerParams(vmem_limit_bytes=40 << 20),
        name="attention_grads",
    )(keep, came)


def matmul(left, right, dims):
    return lax.dot_general(left, right, ((dims[:1], dims[1:]), ((), ())), preferred_element_type=F32)


def on_device(acts, perturb, dy, norm_gain, w_qkv, w_out):
    tensor, member, image = [lax.axis_index(axis) for axis in AXES]
    own_y, core = image // 2, image % 2
    first, stays = core == 0, core == tensor % 2
    features = acts.shape[3]
    heads, head_size = w_qkv.shape[2], w_qkv.shape[4]

    dy_own = swapped(dy[0, 0], stays)

    rows = lax.all_to_all(
        jnp.broadcast_to(perturb, (16, *perturb.shape)), AXES, 0, 0, axis_index_groups=BLOCKS
    )
    rows, dy_own = together(rows, dy_own)
    other = send(rows, CORE)
    shared = jnp.stack([jnp.where(first, rows, other), jnp.where(first, other, rows)], axis=1)
    inputs = acts[0, 0].astype(F32) + shared.reshape(-1, features).astype(F32)
    inputs = inputs.astype(BF)

    raw = w_qkv[0].transpose(0, 2, 1, 3).reshape(-1, head_size)
    w_back = w_out[0].reshape(heads * head_size, features)
    tiles = w_back.reshape(-1, 8, features // 128, 128).transpose(0, 2, 1, 3).reshape(-1, 128)
    eighth = core * 4 + own_y
    piece = jnp.concatenate(
        [
            lax.dynamic_slice_in_dim(array, eighth * (array.shape[0] // 8), array.shape[0] // 8, 0)
            for array in (raw, tiles)
        ],
        axis=0,
    )
    piece, dy_own = together(piece, dy_own)
    piece_other = send(piece, ZL)

    dy_left, dy_right, dy_far = [send(dy_own, X[step]) for step in (1, -1, 2)]
    pieces = [piece_other] + [send(piece_other, Y[step]) for step in (1, -1, 2)]
    in_own = swapped(inputs, stays)
    in_own, raw = together(in_own, raw)
    w_mat = own_weights(raw)
    in_left, in_right, in_far = [send(in_own, X[step]) for step in (1, -1, 2)]
    mat_half, back_half = other_weights(pieces, own_y)

    def halves(mine):
        came = send(mine, CORE)
        return came, [jnp.where(first, mine, came), jnp.where(first, came, mine)]

    w_back_other = jnp.concatenate(halves(back_half)[1], axis=0)
    mat_came, low_high = halves(mat_half)

    rows_dy = jnp.concatenate([dy_own, dy_left, dy_right, dy_far], axis=0)
    normed, rows_in, spread = normed_rows([in_own, in_left, in_right, in_far], norm_gain)
    up = matmul(rows_dy, w_back, (1, 1)).astype(BF)
    packed = matmul(normed, w_mat, (1, 0)).astype(BF)
    up_other = matmul(rows_dy, w_back_other, (1, 1)).astype(BF)
    packed_other = matmul(normed, jnp.concatenate(low_high, axis=0), (1, 0)).astype(BF)
    both = jnp.concatenate([packed, up], axis=1)
    both_other = jnp.concatenate([packed_other, up_other], axis=1)
    keep = jnp.where(first, both, both_other)
    came = send(jnp.where(first, both_other, both), CORE)
    mine, theirs = attention_grads(keep, came)
    came = send(theirs, CORE)
    grads_own = jnp.where(first, mine, came)
    grads_other = jnp.where(first, came, mine)

    w_mat_other = joined(mat_half, mat_came, first)
    partials = [
        lax.optimization_barrier(matmul(grads_own, w_mat, (1, 1)).astype(BF)),
        lax.optimization_barrier(matmul(grads_other, w_mat_other, (1, 1)).astype(BF)),
    ]
    result = result_rows(
        [grads_own, grads_other],
        [packed, packed_other],
        partials,
        rows_in,
        spread,
        norm_gain,
        dy_own,
    )

    def over_x(value):
        count = value.shape[0] // 4
        total = value[:count].astype(F32)
        for place, step in ((3, 2), (1, -1), (2, 1)):
            piece = value[place * count : (place + 1) * count]
            total = total + send(piece, X[step]).astype(F32)
        return total.astype(BF)

    def over(value, ring, own, dim):
        total = lax.dynamic_index_in_dim(value, own, dim, keepdims=False).astype(F32)
        for step in (2, 1, -1):
            piece = lax.dynamic_index_in_dim(value, (own + step) % 4, dim, keepdims=False)
            total = total + send(piece, ring[step]).astype(F32)
        return total

    cut = 1664
    part_a = together(over_x(result[:, :cut]))[0]
    part_b = over(result[:, cut:].reshape(4, 4, 4, 8, -1), Y, own_y, 2).astype(BF)
    part_a = over(part_a.reshape(4, 4, 8, -1), Y, own_y, 1)
    part_b = over_x(part_b.reshape(128, -1)).reshape(4, 8, -1)
    total = jnp.concatenate([part_a.astype(BF), part_b], axis=-1)
    total = over(total, Z, member, 0)
    total = swapped(total, stays).reshape(2, 4, features)
    low, high = total[0], total[1]
    return jnp.where(first, low, high) + send(jnp.where(first, high, low), CORE)


def solution(mesh):
    in_specs = (
        P("member", "image", "tensor", None),
        P(("tensor", "member", "image"), None),
        P("member", "image", "tensor", None),
        P("member", None),
        P("member", None, "tensor", None, None),
        P("member", "tensor", None, None),
    )
    out_specs = P(("tensor", "member", "image"), None)
    return jax.shard_map(
        on_device, mesh=mesh, in_specs=in_specs, out_specs=out_specs, check_vma=False
    )
```

```python
import functools
import math

import jax
import jax.numpy as jnp
from jax import lax
from jax.experimental import pallas as pl
from jax.experimental.pallas import tpu as pltpu
from jax.sharding import PartitionSpec as P

AXES = ("tensor", "member", "image")
BF = jnp.bfloat16
F32 = jnp.float32


def routes(move):
    pairs = []
    for x in range(4):
        for zl in range(2):
            for zh in range(4):
                for y in range(4):
                    for c in range(2):
                        nx, nzl, nzh, ny, nc = move(x, zl, zh, y, c)
                        pairs.append(
                            (
                                ((x * 2 + zl) * 4 + zh) * 8 + y * 2 + c,
                                (((nx % 4) * 2 + nzl) * 4 + nzh % 4) * 8 + (ny % 4) * 2 + nc,
                            )
                        )
    return [(source, target) for source, target in pairs if source != target]


SWAP = routes(lambda x, zl, zh, y, c: (x, c, zh, y, zl))
TURN = routes(lambda x, zl, zh, y, c: (x, c, zh, y, 1 - zl))
CORE = routes(lambda x, zl, zh, y, c: (x, zl, zh, y, 1 - c))
ZL = routes(lambda x, zl, zh, y, c: (x, 1 - zl, zh, y, c))
X = {d: routes(lambda x, zl, zh, y, c, d=d: (x + d, zl, zh, y, c)) for d in (-1, 1, 2)}

Z = {d: routes(lambda x, zl, zh, y, c, d=d: (x, zl, zh + d, y, c)) for d in (-1, 1, 2)}
Y = {d: routes(lambda x, zl, zh, y, c, d=d: (x, zl, zh, y + d, c)) for d in (-1, 1, 2)}


BLOCKS = [
    [(t * 4 + zh) * 8 + y * 2 + c for zh in range(4) for y in range(4)]
    for t in range(8)
    for c in range(2)
]


def send(value, pairs):
    return lax.ppermute(value, AXES, pairs)


def together(*values):
    return lax.optimization_barrier(values)


def swapped(value, stays):
    return jnp.where(stays, value, send(value, SWAP))


def rows_of_weights(raw, scratch, rows):
    scratch[...] = raw.astype(F32)
    return [scratch[pl.ds(column, rows, stride=6), :].astype(BF) for column in range(6)]


def own_weights_body(raw_ref, out_ref, scratch):
    rows = out_ref.shape[0]
    for column, value in enumerate(rows_of_weights(raw_ref[...], scratch, rows)):
        out_ref[:, column * 128 : (column + 1) * 128] = value


def own_weights(raw):
    count, step = raw.shape[0] // 6, 400
    return pl.pallas_call(
        own_weights_body,
        grid=(count // step,),
        in_specs=[pl.BlockSpec((step * 6, 128), lambda i: (i, 0))],
        out_specs=pl.BlockSpec((step, 768), lambda i: (i, 0)),
        out_shape=jax.ShapeDtypeStruct((count, 768), BF),
        scratch_shapes=[pltpu.VMEM((step * 6, 128), F32)],
        compiler_params=pltpu.CompilerParams(vmem_limit_bytes=16 << 20),
        cost_estimate=pl.CostEstimate(flops=0, bytes_accessed=40 << 20, transcendentals=0),
        name="own_weights",
    )(raw)


def other_weights_body(place_ref, p0, p1, p2, p3, mat_ref, back_ref, scratch, scratch_back):
    for ref, step in ((p0, 0), (p1, 3), (p2, 1), (p3, 2)):
        place = (place_ref[0] + step) % 4
        at = pl.multiple_of(place * 400, 16)
        for column, value in enumerate(rows_of_weights(ref[:2400, :], scratch, 400)):
            mat_ref[pl.ds(at, 400), column * 128 : (column + 1) * 128] = value
        scratch_back[...] = ref[2400:, :].astype(F32)
        for pair in range(2):
            row = pl.multiple_of(place * 32 + pair * 16, 16)
            for column in range(25):
                upper = scratch_back[(pair * 50 + column) * 8 : (pair * 50 + column) * 8 + 8, :]
                lower = scratch_back[(pair * 50 + 25 + column) * 8 : (pair * 50 + 25 + column) * 8 + 8, :]
                back_ref[pl.ds(row, 16), column * 128 : (column + 1) * 128] = jnp.concatenate(
                    [upper, lower], axis=0
                ).astype(BF)


def other_weights(pieces, place):
    whole = pl.BlockSpec(memory_space=pltpu.VMEM)
    return pl.pallas_call(
        other_weights_body,
        in_specs=[pl.BlockSpec(memory_space=pltpu.SMEM), whole, whole, whole, whole],
        out_specs=[whole, whole],
        out_shape=[jax.ShapeDtypeStruct((1600, 768), BF), jax.ShapeDtypeStruct((128, 3200), BF)],
        scratch_shapes=[pltpu.VMEM((2400, 128), F32), pltpu.VMEM((800, 128), F32)],
        compiler_params=pltpu.CompilerParams(vmem_limit_bytes=32 << 20),
        cost_estimate=pl.CostEstimate(flops=0, bytes_accessed=40 << 20, transcendentals=0),
        name="other_weights",
    )(place.reshape(1), *pieces)


def normed_body(own, left, right, far, gains_ref, normed_ref, rows_ref, spread_ref):
    start = 0
    for ref in (own, left, right, far):
        for part in range(ref.shape[0] // 64):
            values = ref[part * 64 : part * 64 + 64, :]
            floats = values.astype(F32)
            spread = jnp.sqrt(jnp.mean(floats * floats, axis=-1, keepdims=True) + 1e-06)
            at = slice(start, start + 64)
            normed_ref[at, :] = (floats / spread * gains_ref[...]).astype(BF)
            rows_ref[at, :] = values
            spread_ref[at, :] = jnp.broadcast_to(spread, (64, 128))
            start += 64


def normed_rows(pieces, gains):
    whole = pl.BlockSpec(memory_space=pltpu.VMEM)
    return pl.pallas_call(
        normed_body,
        in_specs=[whole] * 5,
        out_specs=[whole] * 3,
        out_shape=[
            jax.ShapeDtypeStruct((512, 3200), BF),
            jax.ShapeDtypeStruct((512, 3200), BF),
            jax.ShapeDtypeStruct((512, 128), F32),
        ],
        compiler_params=pltpu.CompilerParams(vmem_limit_bytes=16 << 20),
        cost_estimate=pl.CostEstimate(flops=0, bytes_accessed=16 << 20, transcendentals=0),
        name="normed_rows",
    )(*pieces, gains)


def result_body(g_own, g_other, p_own, p_other, part_own, part_other, rows, spread, gains, own_dy, out):
    along = 0.0
    for grads, values in ((g_own, p_own), (g_other, p_other)):
        along = along + jnp.sum(
            grads[...].astype(F32) * values[...].astype(F32), axis=-1, keepdims=True
        )
    inverse = 1.0 / spread[:, :1]
    along = along * inverse * inverse / rows.shape[1]
    is_own = pl.program_id(0) == 0
    tile = 640
    for start in range(0, rows.shape[1], tile):
        at = slice(start, start + tile)
        grad = part_own[:, at].astype(F32) + part_other[:, at].astype(F32)
        value = gains[:, at] * grad * inverse - rows[:, at].astype(F32) * along
        value = value + jnp.where(is_own, own_dy[:, at].astype(F32), 0.0)
        out[:, at] = value.astype(BF)


def result_rows(grads, values, partials, rows, spread, gains, own_dy):
    count, features = rows.shape
    block = own_dy.shape[0]
    narrow = pl.BlockSpec((block, 768), lambda i: (i, 0))
    wide = pl.BlockSpec((block, features), lambda i: (i, 0))
    whole = pl.BlockSpec(memory_space=pltpu.VMEM)
    return pl.pallas_call(
        result_body,
        grid=(count // block,),
        in_specs=[narrow] * 4
        + [wide] * 3
        + [pl.BlockSpec((block, 128), lambda i: (i, 0)), whole, whole],
        out_specs=wide,
        out_shape=jax.ShapeDtypeStruct((count, features), BF),
        compiler_params=pltpu.CompilerParams(vmem_limit_bytes=24 << 20),
        name="result_rows",
    )(*grads, *values, *partials, rows, spread, gains, own_dy)


def joined_body(first_ref, mine, came, out):
    half = mine.shape[0]

    @pl.when(first_ref[0] == 1)
    def _():
        out[:half, :] = mine[...]
        out[half:, :] = came[...]

    @pl.when(first_ref[0] == 0)
    def _():
        out[:half, :] = came[...]
        out[half:, :] = mine[...]


def joined(mine, came, first):
    whole = pl.BlockSpec(memory_space=pltpu.VMEM)
    return pl.pallas_call(
        joined_body,
        in_specs=[pl.BlockSpec(memory_space=pltpu.SMEM), whole, whole],
        out_specs=whole,
        out_shape=jax.ShapeDtypeStruct((2 * mine.shape[0], mine.shape[1]), BF),
        compiler_params=pltpu.CompilerParams(vmem_limit_bytes=32 << 20),
        name="joined",
    )(first.astype(jnp.int32).reshape(1), mine, came)


def attention_body(keep_ref, came_ref, mine_ref, theirs_ref, table, grads, sums):
    half = keep_ref.shape[0]
    rows = 2 * half
    step = 256
    scale = 1.0 / math.sqrt(128)
    table[:half, :] = keep_ref[...]
    table[half:, :] = came_ref[...]
    heads = range(2)
    slots = [[slice(a, a + 128) for a in ((slot * 2 + head) * 128 for slot in range(4))] for head in heads]
    keys_t = [table[:, slots[head][1]].astype(F32).T.astype(BF) for head in heads]
    sums[...] = jnp.zeros_like(sums)

    def block(index, carry):
        here = pl.ds(pl.multiple_of(index * step, step), step)
        query = [table[here, slots[head][0]] for head in heads]
        upstream = [table[here, slots[head][3]] for head in heads]
        scores = [matmul(table[:, slots[head][1]], query[head], (1, 1)) for head in heads]
        through = [matmul(table[:, slots[head][2]], upstream[head], (1, 1)) for head in heads]
        for head in heads:
            expo = jnp.exp((scores[head] - jnp.max(scores[head], axis=0, keepdims=True)) * scale)
            attention = expo * (1.0 / jnp.sum(expo, axis=0, keepdims=True))
            centre = jnp.sum(attention * through[head], axis=0, keepdims=True)
            score_grad = (attention * (through[head] - centre) * scale).astype(BF)
            sums[2 * head] += matmul(score_grad, query[head], (1, 0))
            sums[2 * head + 1] += matmul(attention.astype(BF), upstream[head], (1, 0))
            grads[here, slots[head][0]] = matmul(keys_t[head], score_grad, (1, 0)).T.astype(BF)
        return carry

    lax.fori_loop(0, rows // step, block, 0)
    for head in heads:
        grads[:, slots[head][1]] = sums[2 * head].astype(BF)
        grads[:, slots[head][2]] = sums[2 * head + 1].astype(BF)
    mine_ref[...] = grads[:half, :]
    theirs_ref[...] = grads[half:, :]


def attention_grads(keep, came):
    half = keep.shape[0]
    whole = pl.BlockSpec(memory_space=pltpu.VMEM)
    return pl.pallas_call(
        attention_body,
        in_specs=[whole, whole],
        out_specs=[whole, whole],
        out_shape=[jax.ShapeDtypeStruct((half, 768), BF)] * 2,
        scratch_shapes=[
            pltpu.VMEM((2 * half, 1024), BF),
            pltpu.VMEM((2 * half, 768), BF),
            pltpu.VMEM((4, 2 * half, 128), F32),
        ],
        compiler_params=pltpu.CompilerParams(vmem_limit_bytes=40 << 20),
        name="attention_grads",
    )(keep, came)


def matmul(left, right, dims):
    return lax.dot_general(left, right, ((dims[:1], dims[1:]), ((), ())), preferred_element_type=F32)


def on_device(acts, perturb, dy, norm_gain, w_qkv, w_out):
    tensor, member, image = [lax.axis_index(axis) for axis in AXES]
    own_y, core = image // 2, image % 2
    first, stays = core == 0, core == tensor % 2
    features = acts.shape[3]
    heads, head_size = w_qkv.shape[2], w_qkv.shape[4]

    dy_own = swapped(dy[0, 0], stays)

    rows = lax.all_to_all(
        jnp.broadcast_to(perturb, (16, *perturb.shape)), AXES, 0, 0, axis_index_groups=BLOCKS
    )
    rows, dy_own = together(rows, dy_own)
    other = send(rows, CORE)
    shared = jnp.stack([jnp.where(first, rows, other), jnp.where(first, other, rows)], axis=1)
    inputs = acts[0, 0].astype(F32) + shared.reshape(-1, features).astype(F32)
    inputs = inputs.astype(BF)

    raw = w_qkv[0].transpose(0, 2, 1, 3).reshape(-1, head_size)
    w_back = w_out[0].reshape(heads * head_size, features)
    tiles = w_back.reshape(-1, 8, features // 128, 128).transpose(0, 2, 1, 3).reshape(-1, 128)
    eighth = core * 4 + own_y
    piece = jnp.concatenate(
        [
            lax.dynamic_slice_in_dim(array, eighth * (array.shape[0] // 8), array.shape[0] // 8, 0)
            for array in (raw, tiles)
        ],
        axis=0,
    )
    piece, dy_own = together(piece, dy_own)
    piece_other = send(piece, ZL)

    dy_left, dy_right, dy_far = [send(dy_own, X[step]) for step in (1, -1, 2)]
    pieces = [piece_other] + [send(piece_other, Y[step]) for step in (1, -1, 2)]
    in_own = swapped(inputs, stays)
    in_own, raw = together(in_own, raw)
    w_mat = own_weights(raw)
    in_left, in_right, in_far = [send(in_own, X[step]) for step in (1, -1, 2)]
    mat_half, back_half = other_weights(pieces, own_y)

    def halves(mine):
        came = send(mine, CORE)
        return came, [jnp.where(first, mine, came), jnp.where(first, came, mine)]

    w_back_other = jnp.concatenate(halves(back_half)[1], axis=0)
    mat_came, low_high = halves(mat_half)

    rows_dy = jnp.concatenate([dy_own, dy_left, dy_right, dy_far], axis=0)
    normed, rows_in, spread = normed_rows([in_own, in_left, in_right, in_far], norm_gain)
    up = matmul(rows_dy, w_back, (1, 1)).astype(BF)
    packed = matmul(normed, w_mat, (1, 0)).astype(BF)
    up_other = matmul(rows_dy, w_back_other, (1, 1)).astype(BF)
    packed_other = matmul(normed, jnp.concatenate(low_high, axis=0), (1, 0)).astype(BF)
    both = jnp.concatenate([packed, up], axis=1)
    both_other = jnp.concatenate([packed_other, up_other], axis=1)
    keep = jnp.where(first, both, both_other)
    came = send(jnp.where(first, both_other, both), CORE)
    mine, theirs = attention_grads(keep, came)
    came = send(theirs, CORE)
    grads_own = jnp.where(first, mine, came)
    grads_other = jnp.where(first, came, mine)

    w_mat_other = joined(mat_half, mat_came, first)
    part_other = matmul(grads_other, w_mat_other, (1, 1)).astype(BF)
    part_other, grads_own = together(part_other, grads_own)
    part_own = lax.optimization_barrier(matmul(grads_own, w_mat, (1, 1)).astype(BF))
    partials = [part_own, part_other]
    result = result_rows(
        [grads_own, grads_other],
        [packed, packed_other],
        partials,
        rows_in,
        spread,
        norm_gain,
        dy_own,
    )

    def over_x(value):
        count = value.shape[0] // 4
        total = value[:count].astype(F32)
        for place, step in ((3, 2), (1, -1), (2, 1)):
            piece = value[place * count : (place + 1) * count]
            total = total + send(piece, X[step]).astype(F32)
        return total.astype(BF)

    def over(value, ring, own, dim):
        total = lax.dynamic_index_in_dim(value, own, dim, keepdims=False).astype(F32)
        for step in (2, 1, -1):
            piece = lax.dynamic_index_in_dim(value, (own + step) % 4, dim, keepdims=False)
            total = total + send(piece, ring[step]).astype(F32)
        return total

    cut = 1536
    part_a = together(over_x(result[:, :cut]))[0]
    part_b = over(result[:, cut:].reshape(4, 4, 4, 8, -1), Y, own_y, 2).astype(BF)
    part_a = over(part_a.reshape(4, 4, 8, -1), Y, own_y, 1)
    part_b = over_x(part_b.reshape(128, -1)).reshape(4, 8, -1)
    total = jnp.concatenate([part_a.astype(BF), part_b], axis=-1)
    total = over(total, Z, member, 0)
    total = total.reshape(2, 4, features)
    near = jnp.where(tensor % 2 == 0, total[0], total[1])
    across = jnp.where(tensor % 2 == 0, total[1], total[0])
    return swapped(near, stays) + send(across, TURN)


def solution(mesh):
    in_specs = (
        P("member", "image", "tensor", None),
        P(("tensor", "member", "image"), None),
        P("member", "image", "tensor", None),
        P("member", None),
        P("member", None, "tensor", None, None),
        P("member", "tensor", None, None),
    )
    out_specs = P(("tensor", "member", "image"), None)
    return jax.shard_map(
        on_device, mesh=mesh, in_specs=in_specs, out_specs=out_specs, check_vma=False
    )
```

```python
import functools
import math

import jax
import jax.numpy as jnp
from jax import lax
from jax.experimental import pallas as pl
from jax.experimental.pallas import tpu as pltpu
from jax.sharding import PartitionSpec as P

AXES = ("tensor", "member", "image")
BF = jnp.bfloat16
F32 = jnp.float32


def routes(move):
    pairs = []
    for x in range(4):
        for zl in range(2):
            for zh in range(4):
                for y in range(4):
                    for c in range(2):
                        nx, nzl, nzh, ny, nc = move(x, zl, zh, y, c)
                        pairs.append(
                            (
                                ((x * 2 + zl) * 4 + zh) * 8 + y * 2 + c,
                                (((nx % 4) * 2 + nzl) * 4 + nzh % 4) * 8 + (ny % 4) * 2 + nc,
                            )
                        )
    return [(source, target) for source, target in pairs if source != target]


SWAP = routes(lambda x, zl, zh, y, c: (x, c, zh, y, zl))
CORE = routes(lambda x, zl, zh, y, c: (x, zl, zh, y, 1 - c))
ZL = routes(lambda x, zl, zh, y, c: (x, 1 - zl, zh, y, c))
X = {d: routes(lambda x, zl, zh, y, c, d=d: (x + d, zl, zh, y, c)) for d in (-1, 1, 2)}

Z = {d: routes(lambda x, zl, zh, y, c, d=d: (x, zl, zh + d, y, c)) for d in (-1, 1, 2)}
Y = {d: routes(lambda x, zl, zh, y, c, d=d: (x, zl, zh, y + d, c)) for d in (-1, 1, 2)}


BLOCKS = [
    [(t * 4 + zh) * 8 + y * 2 + c for zh in range(4) for y in range(4)]
    for t in range(8)
    for c in range(2)
]


def send(value, pairs):
    return lax.ppermute(value, AXES, pairs)


def together(*values):
    return lax.optimization_barrier(values)


def swapped(value, stays):
    return jnp.where(stays, value, send(value, SWAP))


def rows_of_weights(raw, scratch, rows):
    scratch[...] = raw.astype(F32)
    return [scratch[pl.ds(column, rows, stride=6), :].astype(BF) for column in range(6)]


def own_weights_body(raw_ref, out_ref, scratch):
    rows = out_ref.shape[0]
    for column, value in enumerate(rows_of_weights(raw_ref[...], scratch, rows)):
        out_ref[:, column * 128 : (column + 1) * 128] = value


def own_weights(raw):
    count, step = raw.shape[0] // 6, 400
    return pl.pallas_call(
        own_weights_body,
        grid=(count // step,),
        in_specs=[pl.BlockSpec((step * 6, 128), lambda i: (i, 0))],
        out_specs=pl.BlockSpec((step, 768), lambda i: (i, 0)),
        out_shape=jax.ShapeDtypeStruct((count, 768), BF),
        scratch_shapes=[pltpu.VMEM((step * 6, 128), F32)],
        compiler_params=pltpu.CompilerParams(vmem_limit_bytes=16 << 20),
        cost_estimate=pl.CostEstimate(flops=0, bytes_accessed=40 << 20, transcendentals=0),
        name="own_weights",
    )(raw)


def other_weights_body(place_ref, p0, p1, p2, p3, mat_ref, back_ref, scratch, scratch_back):
    for ref, step in ((p0, 0), (p1, 3), (p2, 1), (p3, 2)):
        place = (place_ref[0] + step) % 4
        at = pl.multiple_of(place * 400, 16)
        for column, value in enumerate(rows_of_weights(ref[:2400, :], scratch, 400)):
            mat_ref[pl.ds(at, 400), column * 128 : (column + 1) * 128] = value
        scratch_back[...] = ref[2400:, :].astype(F32)
        for pair in range(2):
            row = pl.multiple_of(place * 32 + pair * 16, 16)
            for column in range(25):
                upper = scratch_back[(pair * 50 + column) * 8 : (pair * 50 + column) * 8 + 8, :]
                lower = scratch_back[(pair * 50 + 25 + column) * 8 : (pair * 50 + 25 + column) * 8 + 8, :]
                back_ref[pl.ds(row, 16), column * 128 : (column + 1) * 128] = jnp.concatenate(
                    [upper, lower], axis=0
                ).astype(BF)


def other_weights(pieces, place):
    whole = pl.BlockSpec(memory_space=pltpu.VMEM)
    return pl.pallas_call(
        other_weights_body,
        in_specs=[pl.BlockSpec(memory_space=pltpu.SMEM), whole, whole, whole, whole],
        out_specs=[whole, whole],
        out_shape=[jax.ShapeDtypeStruct((1600, 768), BF), jax.ShapeDtypeStruct((128, 3200), BF)],
        scratch_shapes=[pltpu.VMEM((2400, 128), F32), pltpu.VMEM((800, 128), F32)],
        compiler_params=pltpu.CompilerParams(vmem_limit_bytes=32 << 20),
        cost_estimate=pl.CostEstimate(flops=0, bytes_accessed=40 << 20, transcendentals=0),
        name="other_weights",
    )(place.reshape(1), *pieces)


def normed_body(own, left, right, far, gains_ref, normed_ref, rows_ref, spread_ref):
    start = 0
    for ref in (own, left, right, far):
        for part in range(ref.shape[0] // 64):
            values = ref[part * 64 : part * 64 + 64, :]
            floats = values.astype(F32)
            spread = jnp.sqrt(jnp.mean(floats * floats, axis=-1, keepdims=True) + 1e-06)
            at = slice(start, start + 64)
            normed_ref[at, :] = (floats / spread * gains_ref[...]).astype(BF)
            rows_ref[at, :] = values
            spread_ref[at, :] = jnp.broadcast_to(spread, (64, 128))
            start += 64


def normed_rows(pieces, gains):
    whole = pl.BlockSpec(memory_space=pltpu.VMEM)
    return pl.pallas_call(
        normed_body,
        in_specs=[whole] * 5,
        out_specs=[whole] * 3,
        out_shape=[
            jax.ShapeDtypeStruct((512, 3200), BF),
            jax.ShapeDtypeStruct((512, 3200), BF),
            jax.ShapeDtypeStruct((512, 128), F32),
        ],
        compiler_params=pltpu.CompilerParams(vmem_limit_bytes=16 << 20),
        cost_estimate=pl.CostEstimate(flops=0, bytes_accessed=16 << 20, transcendentals=0),
        name="normed_rows",
    )(*pieces, gains)


def result_body(g_own, g_other, p_own, p_other, part_own, part_other, rows, spread, gains, own_dy, out):
    along = 0.0
    for grads, values in ((g_own, p_own), (g_other, p_other)):
        along = along + jnp.sum(
            grads[...].astype(F32) * values[...].astype(F32), axis=-1, keepdims=True
        )
    inverse = 1.0 / spread[:, :1]
    along = along * inverse * inverse / rows.shape[1]
    is_own = pl.program_id(0) == 0
    tile = 640
    for start in range(0, rows.shape[1], tile):
        at = slice(start, start + tile)
        grad = part_own[:, at].astype(F32) + part_other[:, at].astype(F32)
        value = gains[:, at] * grad * inverse - rows[:, at].astype(F32) * along
        value = value + jnp.where(is_own, own_dy[:, at].astype(F32), 0.0)
        out[:, at] = value.astype(BF)


def result_rows(grads, values, partials, rows, spread, gains, own_dy):
    count, features = rows.shape
    block = own_dy.shape[0]
    narrow = pl.BlockSpec((block, 768), lambda i: (i, 0))
    wide = pl.BlockSpec((block, features), lambda i: (i, 0))
    whole = pl.BlockSpec(memory_space=pltpu.VMEM)
    return pl.pallas_call(
        result_body,
        grid=(count // block,),
        in_specs=[narrow] * 4
        + [wide] * 3
        + [pl.BlockSpec((block, 128), lambda i: (i, 0)), whole, whole],
        out_specs=wide,
        out_shape=jax.ShapeDtypeStruct((count, features), BF),
        compiler_params=pltpu.CompilerParams(vmem_limit_bytes=24 << 20),
        name="result_rows",
    )(*grads, *values, *partials, rows, spread, gains, own_dy)


def joined_body(first_ref, mine, came, out):
    half = mine.shape[0]

    @pl.when(first_ref[0] == 1)
    def _():
        out[:half, :] = mine[...]
        out[half:, :] = came[...]

    @pl.when(first_ref[0] == 0)
    def _():
        out[:half, :] = came[...]
        out[half:, :] = mine[...]


def joined(mine, came, first):
    whole = pl.BlockSpec(memory_space=pltpu.VMEM)
    return pl.pallas_call(
        joined_body,
        in_specs=[pl.BlockSpec(memory_space=pltpu.SMEM), whole, whole],
        out_specs=whole,
        out_shape=jax.ShapeDtypeStruct((2 * mine.shape[0], mine.shape[1]), BF),
        compiler_params=pltpu.CompilerParams(vmem_limit_bytes=32 << 20),
        name="joined",
    )(first.astype(jnp.int32).reshape(1), mine, came)


def attention_body(keep_ref, came_ref, mine_ref, theirs_ref, table, grads, sums):
    half = keep_ref.shape[0]
    rows = 2 * half
    step = 256
    scale = 1.0 / math.sqrt(128)
    table[:half, :] = keep_ref[...]
    table[half:, :] = came_ref[...]
    heads = range(2)
    slots = [[slice(a, a + 128) for a in ((slot * 2 + head) * 128 for slot in range(4))] for head in heads]
    keys_t = [table[:, slots[head][1]].astype(F32).T.astype(BF) for head in heads]
    sums[...] = jnp.zeros_like(sums)

    def block(index, carry):
        here = pl.ds(pl.multiple_of(index * step, step), step)
        query = [table[here, slots[head][0]] for head in heads]
        upstream = [table[here, slots[head][3]] for head in heads]
        scores = [matmul(table[:, slots[head][1]], query[head], (1, 1)) for head in heads]
        through = [matmul(table[:, slots[head][2]], upstream[head], (1, 1)) for head in heads]
        for head in heads:
            expo = jnp.exp((scores[head] - jnp.max(scores[head], axis=0, keepdims=True)) * scale)
            attention = expo * (1.0 / jnp.sum(expo, axis=0, keepdims=True))
            centre = jnp.sum(attention * through[head], axis=0, keepdims=True)
            score_grad = (attention * (through[head] - centre) * scale).astype(BF)
            sums[2 * head] += matmul(score_grad, query[head], (1, 0))
            sums[2 * head + 1] += matmul(attention.astype(BF), upstream[head], (1, 0))
            grads[here, slots[head][0]] = matmul(keys_t[head], score_grad, (1, 0)).T.astype(BF)
        return carry

    lax.fori_loop(0, rows // step, block, 0)
    for head in heads:
        grads[:, slots[head][1]] = sums[2 * head].astype(BF)
        grads[:, slots[head][2]] = sums[2 * head + 1].astype(BF)
    mine_ref[...] = grads[:half, :]
    theirs_ref[...] = grads[half:, :]


def attention_grads(keep, came):
    half = keep.shape[0]
    whole = pl.BlockSpec(memory_space=pltpu.VMEM)
    return pl.pallas_call(
        attention_body,
        in_specs=[whole, whole],
        out_specs=[whole, whole],
        out_shape=[jax.ShapeDtypeStruct((half, 768), BF)] * 2,
        scratch_shapes=[
            pltpu.VMEM((2 * half, 1024), BF),
            pltpu.VMEM((2 * half, 768), BF),
            pltpu.VMEM((4, 2 * half, 128), F32),
        ],
        compiler_params=pltpu.CompilerParams(vmem_limit_bytes=40 << 20),
        name="attention_grads",
    )(keep, came)


def matmul(left, right, dims):
    return lax.dot_general(left, right, ((dims[:1], dims[1:]), ((), ())), preferred_element_type=F32)


def on_device(acts, perturb, dy, norm_gain, w_qkv, w_out):
    tensor, member, image = [lax.axis_index(axis) for axis in AXES]
    own_y, core = image // 2, image % 2
    first, stays = core == 0, core == tensor % 2
    features = acts.shape[3]
    heads, head_size = w_qkv.shape[2], w_qkv.shape[4]

    dy_own = swapped(dy[0, 0], stays)

    rows = lax.all_to_all(
        jnp.broadcast_to(perturb, (16, *perturb.shape)), AXES, 0, 0, axis_index_groups=BLOCKS
    )
    rows, dy_own = together(rows, dy_own)
    other = send(rows, CORE)
    shared = jnp.stack([jnp.where(first, rows, other), jnp.where(first, other, rows)], axis=1)
    inputs = acts[0, 0].astype(F32) + shared.reshape(-1, features).astype(F32)
    inputs = inputs.astype(BF)

    raw = w_qkv[0].transpose(0, 2, 1, 3).reshape(-1, head_size)
    w_back = w_out[0].reshape(heads * head_size, features)
    tiles = w_back.reshape(-1, 8, features // 128, 128).transpose(0, 2, 1, 3).reshape(-1, 128)
    eighth = core * 4 + own_y
    piece = jnp.concatenate(
        [
            lax.dynamic_slice_in_dim(array, eighth * (array.shape[0] // 8), array.shape[0] // 8, 0)
            for array in (raw, tiles)
        ],
        axis=0,
    )
    piece, dy_own = together(piece, dy_own)
    piece_other = send(piece, ZL)

    dy_left, dy_right, dy_far = [send(dy_own, X[step]) for step in (1, -1, 2)]
    pieces = [piece_other] + [send(piece_other, Y[step]) for step in (1, -1, 2)]
    in_own = swapped(inputs, stays)
    in_own, raw = together(in_own, raw)
    w_mat = own_weights(raw)
    in_left, in_right, in_far = [send(in_own, X[step]) for step in (1, -1, 2)]
    mat_half, back_half = other_weights(pieces, own_y)

    def halves(mine):
        came = send(mine, CORE)
        return came, [jnp.where(first, mine, came), jnp.where(first, came, mine)]

    w_back_other = jnp.concatenate(halves(back_half)[1], axis=0)
    mat_came, low_high = halves(mat_half)

    rows_dy = jnp.concatenate([dy_own, dy_left, dy_right, dy_far], axis=0)
    normed, rows_in, spread = normed_rows([in_own, in_left, in_right, in_far], norm_gain)
    up = matmul(rows_dy, w_back, (1, 1)).astype(BF)
    packed = matmul(normed, w_mat, (1, 0)).astype(BF)
    up_other = matmul(rows_dy, w_back_other, (1, 1)).astype(BF)
    packed_other = matmul(normed, jnp.concatenate(low_high, axis=0), (1, 0)).astype(BF)
    both = jnp.concatenate([packed, up], axis=1)
    both_other = jnp.concatenate([packed_other, up_other], axis=1)
    keep = jnp.where(first, both, both_other)
    came = send(jnp.where(first, both_other, both), CORE)
    mine, theirs = attention_grads(keep, came)
    came = send(theirs, CORE)
    grads_own = jnp.where(first, mine, came)
    grads_other = jnp.where(first, came, mine)

    w_mat_other = joined(mat_half, mat_came, first)
    part_other = matmul(grads_other, w_mat_other, (1, 1)).astype(BF)
    part_other, grads_own = together(part_other, grads_own)
    part_own = lax.optimization_barrier(matmul(grads_own, w_mat, (1, 1)).astype(BF))
    partials = [part_own, part_other]
    result = result_rows(
        [grads_own, grads_other],
        [packed, packed_other],
        partials,
        rows_in,
        spread,
        norm_gain,
        dy_own,
    )

    def over_x(value):
        count = value.shape[0] // 4
        total = value[:count].astype(F32)
        for place, step in ((3, 2), (1, -1), (2, 1)):
            piece = value[place * count : (place + 1) * count]
            total = total + send(piece, X[step]).astype(F32)
        return total.astype(BF)

    def over(value, ring, own, dim):
        total = lax.dynamic_index_in_dim(value, own, dim, keepdims=False).astype(F32)
        for step in (2, 1, -1):
            piece = lax.dynamic_index_in_dim(value, (own + step) % 4, dim, keepdims=False)
            total = total + send(piece, ring[step]).astype(F32)
        return total

    cut = 1664
    part_a = together(over_x(result[:, :cut]))[0]
    part_b = over(result[:, cut:].reshape(4, 4, 4, 8, -1), Y, own_y, 2).astype(BF)
    part_a = over(part_a.reshape(4, 4, 8, -1), Y, own_y, 1)
    part_b = over_x(part_b.reshape(128, -1)).reshape(4, 8, -1)
    total = jnp.concatenate([part_a.astype(BF), part_b], axis=-1)
    total = over(total, Z, member, 0)
    total = swapped(total, stays).reshape(2, 4, features)
    low, high = total[0], total[1]
    return jnp.where(first, low, high) + send(jnp.where(first, high, low), CORE)


def solution(mesh):
    in_specs = (
        P("member", "image", "tensor", None),
        P(("tensor", "member", "image"), None),
        P("member", "image", "tensor", None),
        P("member", None),
        P("member", None, "tensor", None, None),
        P("member", "tensor", None, None),
    )
    out_specs = P(("tensor", "member", "image"), None)
    return jax.shard_map(
        on_device, mesh=mesh, in_specs=in_specs, out_specs=out_specs, check_vma=False
    )
```
